256 devices in a mesh: context: 64 (over x, y_lo, z), dp: 4 (over y_hi, core).
Axes of the slice: x: 4, y: 4 (y_hi: 2, y_lo: 2; y = y_hi * 2 + y_lo), z: 8, core: 2. Of those that a mesh axis runs over, the one named last changes fastest.
Arguments:
- queries: bfloat16 [4, 8192, 1024], P('dp', 'context'), may hold values from -12 to 12
- key_states: bfloat16 [4, 8192, 128], P('dp', 'context'), may hold values from -12 to 12
- value_states: bfloat16 [4, 8192, 128], P('dp', 'context'), may hold values from -6 to 6
- attn_out: bfloat16 [4, 8192, 1024], P('dp', 'context'), may hold values from -6 to 6
- out_grad: bfloat16 [4, 8192, 1024], P('dp', 'context'), may hold values from -6 to 6
- activations: bfloat16 [4, 8192, 8192], P('dp', 'context'), may hold values from -6 to 6
- segment_ids: int32 [4, 8192], P('dp', 'context'), may hold values from 0 to 3, as said below
- span_order: int32 [128], replicated, may hold values from 0 to 127, as said below
- kv_weight: float32 [2, 8192, 128], P(None, ('context', 'dp')), may hold values from -40 to 40
- moment_one: float32 [2, 8192, 128], P(None, ('context', 'dp')), may hold values from -200 to 200
- moment_two: float32 [2, 8192, 128], P(None, ('context', 'dp')), may hold values from 2 to 20000
Outputs:
- query_grad: bfloat16 [4, 8192, 1024], P('dp', 'context')
- kv_grad: bfloat16 [4, 8192, 256], P('dp', 'context')
- new_weight: float32 [2, 8192, 128], P(None, ('context', 'dp'))
- new_moment_one: float32 [2, 8192, 128], P(None, ('context', 'dp'))
- new_moment_two: float32 [2, 8192, 128], P(None, ('context', 'dp'))
- trust_ratio: float32 [2], replicated
The draws below stay inside these ranges and needn't reach their ends.
Inputs may be any that keep to these rules, and one draw needn't show every extreme that they name: `span_order`: stored spans 2i and 2i+1 hold the sequence's spans p and 127 - p, each span exactly once. `segment_ids`: along positions the ids never fall; every sequence holds ids 0 to 3; the document of the last position holds 8 positions or more.
All inputs are finite; a program needn't handle non-finite values.
Results may differ from the reference program's by a relative error of at most 0.0055.
Values may be sent and summed in bfloat16 or wider, within the bound.
A program may use at most 64 MiB of HBM per device.

```python
import jax
import jax.numpy as jnp
from jax import lax

D = 8192
HEADS = 8
HEAD_DIM = 128
SEQ_DEV = 128
SEQ_LEN = 8192
SEQS = 4
N_CONTEXT = 64


def paired_order(key):
    key = jax.random.fold_in(key, 11)
    lower = jax.random.permutation(key, N_CONTEXT).astype(jnp.int32)
    upper = (2 * N_CONTEXT - 1 - lower).astype(jnp.int32)
    return jnp.stack([lower, upper], axis=1).reshape(2 * N_CONTEXT)


def layout_row(order, position):
    half = SEQ_DEV // 2
    inverse = jnp.argsort(order, stable=True).astype(jnp.int32)
    return inverse[position // half] * half + position % half


def drawn_rows(key):
    order = paired_order(key)
    position = (SEQ_LEN - 1 - 2 * jnp.arange(4, dtype=jnp.int32)).astype(jnp.int32)
    own_rows = layout_row(order, position)
    before_rows = layout_row(order, position - 1)
    return (own_rows, before_rows)


def blend_rows(base, rows_at):
    current = base[:, rows_at, :]
    return base.at[:, rows_at, :].set(current)


def draw_span_order(key, part):
    return paired_order(key)


def draw_segment_ids(key, part):
    order = paired_order(key)
    key = jax.random.fold_in(key, 5)
    half = SEQ_DEV // 2
    layout = jnp.arange(SEQ_LEN, dtype=jnp.int32)
    position = order[layout // half] * half + layout % half

    def single(subkey):
        cut_points = jax.random.permutation(subkey, SEQ_LEN - 8)[:3].astype(jnp.int32) + 1
        return jnp.sum((position[:, None] >= cut_points[None, :]).astype(jnp.int32), axis=1)
    return jax.vmap(single)(jax.random.split(key, SEQS)).astype(jnp.int32)


def draw_queries(key, part):
    own_rows, before_rows = drawn_rows(key)
    key = jax.random.fold_in(key, 1)
    shape = (SEQS, SEQ_LEN, HEADS * HEAD_DIM)
    base = jnp.clip(jax.random.normal(key, shape, jnp.float32), -4.0, 4.0)
    return blend_rows(base, own_rows).astype(jnp.bfloat16)


def draw_key_states(key, part):
    own_rows, before_rows = drawn_rows(key)
    key = jax.random.fold_in(key, 2)
    shape = (SEQS, SEQ_LEN, HEAD_DIM)
    base = jnp.clip(jax.random.normal(key, shape, jnp.float32), -4.0, 4.0)
    base = blend_rows(base, own_rows)
    return blend_rows(base, before_rows).astype(jnp.bfloat16)


def scaled_field(key, factor):
    first, second = jax.random.split(key)
    level = jnp.arange(D, dtype=jnp.float32) / D
    row_scale = jnp.power(10.0, level)
    column_scale = jnp.power(10.0, jax.random.uniform(second, (2, 1, HEAD_DIM), jnp.float32))
    return (first, factor * row_scale[None, :, None] * column_scale)


def draw_kv_weight(key, part):
    key = jax.random.fold_in(key, 21)
    noise_key, scale = scaled_field(key, 0.1)
    noise = jnp.clip(jax.random.normal(noise_key, (2, D, HEAD_DIM), jnp.float32), -4.0, 4.0)
    return noise * scale


def draw_moment_one(key, part):
    key = jax.random.fold_in(key, 22)
    noise_key, scale = scaled_field(key, 0.5)
    noise = jnp.clip(jax.random.normal(noise_key, (2, D, HEAD_DIM), jnp.float32), -4.0, 4.0)
    return noise * scale


def draw_moment_two(key, part):
    key = jax.random.fold_in(key, 23)
    noise_key, scale = scaled_field(key, 20.0)
    spread = jax.random.uniform(noise_key, (2, D, HEAD_DIM), jnp.float32, -1.0, 1.0)
    return jnp.power(10.0, spread) * scale


def block_scale(own_key, extent, cuts, low, high):
    gain, own = 1.0, jax.random.fold_in(own_key, 6)
    for dim, blocks in cuts:
        heights = jnp.exp(jax.random.uniform(jax.random.fold_in(own, dim), (blocks,), jnp.float32, low / len(cuts), high / len(cuts)))
        gain = gain * jnp.repeat(heights, extent[dim] // blocks).reshape([-1 if axis == dim else 1 for axis in range(len(extent))])
    return gain


def gaussian(stream_key, shape, scale, most, cuts=(), held_as=jnp.bfloat16):
    values = jax.random.normal(stream_key, shape, jnp.float32) * scale
    if len(cuts) > 0:
        values = block_scale(stream_key, shape, cuts, -0.22, 0.18) * values
    return jnp.clip(values, min=-most, max=most).astype(held_as)


def setup_inputs(seed: int = 0) -> dict:
    streams_of = jax.random.split(jax.random.key(seed), 12)
    return {
        "queries": draw_queries(jax.random.fold_in(streams_of[11], 71), 0),
        "key_states": draw_key_states(jax.random.fold_in(streams_of[11], 71), 0),
        "value_states": gaussian(streams_of[2], (SEQS, SEQ_LEN, HEAD_DIM), 1.0, 6.0, ((0, 4), (1, 64))),
        "attn_out": gaussian(streams_of[3], (SEQS, SEQ_LEN, HEADS * HEAD_DIM), 1.0, 6.0, ((0, 4), (1, 64))),
        "out_grad": gaussian(streams_of[4], (SEQS, SEQ_LEN, HEADS * HEAD_DIM), 1.0, 6.0, ((0, 4), (1, 64))),
        "activations": gaussian(streams_of[5], (SEQS, SEQ_LEN, D), 1.0, 6.0, ((0, 4), (1, 64))),
        "segment_ids": draw_segment_ids(jax.random.fold_in(streams_of[11], 71), 0),
        "span_order": draw_span_order(jax.random.fold_in(streams_of[11], 71), 0),
        "kv_weight": draw_kv_weight(jax.random.fold_in(streams_of[11], 71), 0),
        "moment_one": draw_moment_one(jax.random.fold_in(streams_of[11], 71), 0),
        "moment_two": draw_moment_two(jax.random.fold_in(streams_of[11], 71), 0),
    }


beta_one = 0.9
beta_two = 0.999
epsilon = 1e-06
weight_decay = 0.01
learn_rate = 0.01

def layout_positions(span_order):
    half = SEQ_DEV // 2
    layout = jnp.arange(SEQ_LEN, dtype=jnp.int32)
    return span_order[layout // half] * half + layout % half

def rounded(values):
    return lax.optimization_barrier(values.astype(jnp.bfloat16)).astype(jnp.float32)

def one_sequence(position, queries, key_states, value_states, attn_out, out_grad, segment):
    score_scale = HEAD_DIM ** (-0.5)
    query_all = queries.astype(jnp.float32).reshape(SEQ_LEN, HEADS, HEAD_DIM)
    grad_all = out_grad.astype(jnp.float32).reshape(SEQ_LEN, HEADS, HEAD_DIM)
    output_all = attn_out.astype(jnp.float32).reshape(SEQ_LEN, HEADS, HEAD_DIM)
    delta_all = lax.optimization_barrier(jnp.sum(grad_all * output_all, axis=2))
    key_float = key_states.astype(jnp.float32)
    value_float = value_states.astype(jnp.float32)

    def query_block_step(running, first_row):
        query_block = lax.dynamic_slice_in_dim(query_all, first_row, SEQ_DEV, 0)
        grad_block = lax.dynamic_slice_in_dim(grad_all, first_row, SEQ_DEV, 0)
        delta_block = lax.dynamic_slice_in_dim(delta_all, first_row, SEQ_DEV, 0)
        query_place = lax.dynamic_slice_in_dim(position, first_row, SEQ_DEV, 0)
        query_segment = lax.dynamic_slice_in_dim(segment, first_row, SEQ_DEV, 0)
        visible = (position[None, :] <= query_place[:, None]) & (segment[None, :] == query_segment[:, None])
        visible = visible[:, None, :]
        scores = jnp.einsum('qhd,kd->qhk', query_block, key_float) * score_scale
        masked = jnp.where(visible, scores, -jnp.inf)
        row_top = lax.optimization_barrier(jnp.max(masked, axis=2, keepdims=True))
        log_total = row_top + jnp.log(lax.optimization_barrier(jnp.sum(jnp.exp(masked - row_top), axis=2, keepdims=True)))
        probs = jnp.where(visible, jnp.exp(scores - log_total), 0.0)
        prob_grad = jnp.einsum('qhd,kd->qhk', grad_block, value_float)
        score_grad = rounded(score_scale * probs * (prob_grad - delta_block[:, :, None]))
        query_grad = jnp.einsum('qhk,kd->qhd', score_grad, key_float)
        key_grad = jnp.einsum('qhk,qhd->kd', score_grad, query_block)
        value_grad = jnp.einsum('qhk,qhd->kd', rounded(probs), grad_block)
        running = running + jnp.concatenate([key_grad, value_grad], axis=1)
        return (running, query_grad.reshape(SEQ_DEV, HEADS * HEAD_DIM).astype(jnp.bfloat16))
    starts = jnp.arange(0, SEQ_LEN, SEQ_DEV, dtype=jnp.int32)
    initial = jnp.zeros((SEQ_LEN, 2 * HEAD_DIM), jnp.float32)
    kv_float, query_grads = lax.scan(query_block_step, initial, starts)
    return (kv_float.astype(jnp.bfloat16), query_grads.reshape(SEQ_LEN, HEADS * HEAD_DIM))

def reference(queries, key_states, value_states, attn_out, out_grad, activations, segment_ids, span_order, kv_weight, moment_one, moment_two):
    position = layout_positions(span_order)
    kv_list = []
    query_list = []
    gradient = jnp.zeros((D, 2 * HEAD_DIM), jnp.float32)
    for sequence in range(SEQS):
        kv_low, query_grad = one_sequence(position, queries[sequence], key_states[sequence], value_states[sequence], attn_out[sequence], out_grad[sequence], segment_ids[sequence])
        kv_list.append(kv_low)
        query_list.append(query_grad)
        gradient = gradient + lax.dot_general(activations[sequence], kv_low, (((0,), (0,)), ((), ())), preferred_element_type=jnp.float32)
    gradient = jnp.stack([gradient[:, :HEAD_DIM], gradient[:, HEAD_DIM:]])
    new_one = beta_one * moment_one + (1.0 - beta_one) * gradient
    new_two = beta_two * moment_two + (1.0 - beta_two) * gradient * gradient
    update = new_one / (jnp.sqrt(new_two) + epsilon) + weight_decay * kv_weight
    weight_norm = jnp.sqrt(lax.optimization_barrier(jnp.sum(kv_weight * kv_weight, axis=(1, 2))))
    update_norm = jnp.sqrt(lax.optimization_barrier(jnp.sum(update * update, axis=(1, 2))))
    trust_ratio = weight_norm / (update_norm + epsilon)
    new_weight = kv_weight - learn_rate * trust_ratio[:, None, None] * update
    return (jnp.stack(query_list), jnp.stack(kv_list), new_weight, new_one, new_two, trust_ratio)
```

```python
import functools

import jax
import jax.numpy as jnp
from jax import lax
from jax.experimental import pallas as pl
from jax.experimental.pallas import tpu as pltpu
from jax.sharding import PartitionSpec as P

beta_one = 0.9
beta_two = 0.999
epsilon = 1e-06
weight_decay = 0.01
learn_rate = 0.01

HEADS = 8
DIM = 128
SPAN = 64
ROWS = 128
LANES = HEADS * SPAN
BLOCK = 256
KEYS = 2048
SCALE = DIM ** (-0.5)
LOG2E = 1.4426950408889634
MESH = pl.DeviceIdType.MESH
VMEM = pltpu.VMEM
F32 = jnp.float32
BF16 = jnp.bfloat16


def vmem_spec():
    return pl.BlockSpec(memory_space=pltpu.VMEM)


def any_spec():
    return pl.BlockSpec(memory_space=pl.ANY)


def smem_spec():
    return pl.BlockSpec(memory_space=pltpu.SMEM)


def greet(peers):
    barrier = pltpu.get_barrier_semaphore()
    for peer in peers:
        pl.semaphore_signal(barrier, inc=1, device_id=peer, device_id_type=MESH)
    return barrier


def send(src, dst, send_sem, recv_sem, peer):
    copy = pltpu.make_async_remote_copy(
        src_ref=src, dst_ref=dst, send_sem=send_sem, recv_sem=recv_sem,
        device_id=peer, device_id_type=MESH,
    )
    copy.start()
    return copy


def arrived(dst, sem):
    pltpu.make_async_copy(dst, dst, sem).wait()


def place():
    me = lax.axis_index("context")
    dp = lax.axis_index("dp")
    return me, dp, me // 16, me % 16


def x_peers(me, dp, x, rest):
    return [(lax.rem(x + i, 4) * 16 + rest, dp) for i in range(1, 4)]


def rest_peers(me, dp, x, rest):
    return [(x * 16 + lax.rem(rest + i, 16), dp) for i in range(1, 16)]


def gather_kernel(
    q_ref, g_ref, o_ref, k_ref, v_ref, seg_ref, segk_ref,
    qg_ref, gg_ref, kvg_ref, auxg_ref, segg_ref,
    qbuf, gbuf, kvbuf, auxbuf,
    x_send, x_recv, r_send, r_recv, own_sem,
):
    me, dp, x, rest = place()
    xs = x_peers(me, dp, x, rest)
    rs = rest_peers(me, dp, x, rest)
    barrier = greet(xs + rs)
    kvbuf[0] = k_ref[...]
    kvbuf[1] = v_ref[...]
    for span in range(2):
        rows = pl.ds(span * SPAN, SPAN)
        pieces = []
        for h in range(HEADS):
            cols = pl.ds(h * DIM, DIM)
            qbuf[span, pl.ds(h * SPAN, SPAN), :] = q_ref[rows, cols]
            grad = g_ref[rows, cols]
            gbuf[span, pl.ds(h * SPAN, SPAN), :] = grad
            pieces.append(grad.astype(F32) * o_ref[rows, cols].astype(F32))
        product = jnp.concatenate(pieces, axis=0)
        auxbuf[pl.ds(span, 1), :] = jnp.sum(product.T, axis=0, keepdims=True)
    auxbuf[pl.ds(2, 2), :] = seg_ref[...]
    auxbuf[pl.ds(4, 4), :] = jnp.zeros((4, LANES), F32)
    pl.semaphore_wait(barrier, len(xs) + len(rs))
    copies = []
    two = pl.ds(2 * x, 2)
    for i, peer in enumerate(rs):
        copies.append(send(kvbuf, kvg_ref.at[rest], r_send.at[0, i], r_recv.at[0, rest], peer))
        copies.append(send(segk_ref, segg_ref.at[rest], r_send.at[1, i], r_recv.at[1, rest], peer))
        if i < 3:
            copies.append(send(qbuf, qg_ref.at[two], x_send.at[0, i], x_recv.at[0, x], xs[i]))
            copies.append(send(gbuf, gg_ref.at[two], x_send.at[1, i], x_recv.at[1, x], xs[i]))
            copies.append(send(auxbuf, auxg_ref.at[x], x_send.at[2, i], x_recv.at[2, x], xs[i]))
    own = [
        pltpu.make_async_copy(kvbuf, kvg_ref.at[rest], own_sem.at[0]),
        pltpu.make_async_copy(segk_ref, segg_ref.at[rest], own_sem.at[1]),
        pltpu.make_async_copy(qbuf, qg_ref.at[two], own_sem.at[2]),
        pltpu.make_async_copy(gbuf, gg_ref.at[two], own_sem.at[3]),
        pltpu.make_async_copy(auxbuf, auxg_ref.at[x], own_sem.at[4]),
    ]
    for copy in own:
        copy.start()
    for copy in own:
        copy.wait()
    for i in range(1, 16):
        slot = lax.rem(rest + i, 16)
        arrived(kvg_ref.at[slot], r_recv.at[0, slot])
        arrived(segg_ref.at[slot], r_recv.at[1, slot])
    for i in range(1, 4):
        slot = lax.rem(x + i, 4)
        pair = pl.ds(2 * slot, 2)
        arrived(qg_ref.at[pair], x_recv.at[0, slot])
        arrived(gg_ref.at[pair], x_recv.at[1, slot])
        arrived(auxg_ref.at[slot], x_recv.at[2, slot])
    for copy in copies:
        copy.wait_send()


def gather(queries, out_grad, attn_out, key_states, value_states, seg_rows, seg_keys):
    return pl.pallas_call(
        gather_kernel,
        out_shape=(
            jax.ShapeDtypeStruct((8, LANES, DIM), BF16),
            jax.ShapeDtypeStruct((8, LANES, DIM), BF16),
            jax.ShapeDtypeStruct((16, 2, ROWS, DIM), BF16),
            jax.ShapeDtypeStruct((4, 8, LANES), F32),
            jax.ShapeDtypeStruct((16, 8, ROWS), F32),
        ),
        in_specs=[vmem_spec()] * 7,
        out_specs=(any_spec(),) * 5,
        scratch_shapes=[
            VMEM((2, LANES, DIM), BF16),
            VMEM((2, LANES, DIM), BF16),
            VMEM((2, ROWS, DIM), BF16),
            VMEM((8, LANES), F32),
            pltpu.SemaphoreType.DMA((3, 3)),
            pltpu.SemaphoreType.DMA((3, 4)),
            pltpu.SemaphoreType.DMA((2, 15)),
            pltpu.SemaphoreType.DMA((2, 16)),
            pltpu.SemaphoreType.DMA((5,)),
        ],
        compiler_params=pltpu.CompilerParams(
            collective_id=0, has_side_effects=True, vmem_limit_bytes=32 * 1024 * 1024
        ),
        name="gather_rows",
    )(queries, out_grad, attn_out, key_states, value_states, seg_rows, seg_keys)


def key_counts(segg_ref):
    seg = segg_ref[:, 0, :]
    return [jnp.sum((seg < d - 0.5).astype(F32)).astype(jnp.int32) for d in (1, 2, 3)]


def span_range(meta_ref, auxg_ref, counts, s):
    slot = s // 2
    seg = auxg_ref[slot, pl.ds(2 + s % 2, 1), :]
    low = jnp.where(
        seg > 2.5, counts[2], jnp.where(seg > 1.5, counts[1], jnp.where(seg > 0.5, counts[0], 0))
    )
    x = lax.axis_index("context") // 16
    own = (slot == x).astype(jnp.int32)
    base = meta_ref[32 + s] * SPAN
    row = lax.broadcasted_iota(jnp.int32, (1, LANES), 1) % SPAN
    high = base + own * (row + 1)
    low_min, low_max = jnp.min(low), jnp.max(low)
    high_min, high_max = base + own, base + own * SPAN
    first = low_min // BLOCK
    last = (high_max + BLOCK - 1) // BLOCK
    return low, high, low_max, high_min, first, last


def inside(low, high, block):
    place_of = block * BLOCK + lax.broadcasted_iota(jnp.int32, (BLOCK, LANES), 0)
    return (place_of >= low) & (place_of < high)


def sort_keys(meta_ref, kvg_ref, which, sorted_ref):
    def step(t, carry):
        rank = meta_ref[t]
        source = pl.multiple_of((t % 2) * SPAN, SPAN)
        target = pl.multiple_of(rank * SPAN, SPAN)
        sorted_ref[pl.ds(target, SPAN), :] = kvg_ref[t // 2, which, pl.ds(source, SPAN), :]
        return carry

    lax.fori_loop(0, 32, step, 0)


def stats_kernel(meta_ref, qg_ref, kvg_ref, auxg_ref, segg_ref, out_ref, ks, qt, top, total):
    sort_keys(meta_ref, kvg_ref, 0, ks)
    counts = key_counts(segg_ref)

    def span_step(s, carry):
        low, high, low_max, high_min, first, last = span_range(meta_ref, auxg_ref, counts, s)
        qt[...] = qg_ref[s].T
        top[...] = jnp.full((1, LANES), -1e30, F32)
        total[...] = jnp.zeros((1, LANES), F32)

        def tile(block, masked):
            offset = pl.multiple_of(block * BLOCK, BLOCK)
            scores = jnp.dot(
                ks[pl.ds(offset, BLOCK), :], qt[...], preferred_element_type=F32
            ) * (SCALE * LOG2E)
            if masked:
                seen = inside(low, high, block)
                scores = jnp.where(seen, scores, -1e30)
            old = top[...]
            new = jnp.maximum(old, jnp.max(scores, axis=0, keepdims=True))
            weights = jnp.exp2(scores - new)
            if masked:
                weights = jnp.where(seen, weights, 0.0)
            total[...] = total[...] * jnp.exp2(old - new) + jnp.sum(weights, axis=0, keepdims=True)
            top[...] = new

        def block_step(block, carry):
            edge = (block * BLOCK < low_max) | ((block + 1) * BLOCK > high_min)

            @pl.when(edge)
            def _():
                tile(block, True)

            @pl.when(jnp.logical_not(edge))
            def _():
                tile(block, False)

            return carry

        lax.fori_loop(first, last, block_step, 0)
        out_ref[0, pl.ds(s, 1), :] = top[...]
        out_ref[1, pl.ds(s, 1), :] = total[...]
        return carry

    lax.fori_loop(0, 8, span_step, 0)


def stats(meta, qg, kvg, auxg, segg):
    return pl.pallas_call(
        stats_kernel,
        out_shape=jax.ShapeDtypeStruct((2, 8, LANES), F32),
        in_specs=[smem_spec()] + [vmem_spec()] * 4,
        out_specs=vmem_spec(),
        scratch_shapes=[
            VMEM((KEYS, DIM), BF16),
            VMEM((DIM, LANES), BF16),
            VMEM((1, LANES), F32),
            VMEM((1, LANES), F32),
        ],
        compiler_params=pltpu.CompilerParams(vmem_limit_bytes=48 * 1024 * 1024),
        name="softmax_totals",
    )(meta, qg, kvg, auxg, segg)


def combine_kernel(part_ref, out_ref, got, send_sem, recv_sem):
    me, dp, x, rest = place()
    xs = x_peers(me, dp, x, rest)
    barrier = greet(xs)
    got[x] = part_ref[...]
    pl.semaphore_wait(barrier, len(xs))
    copies = [
        send(part_ref, got.at[x], send_sem.at[i], recv_sem.at[x], peer)
        for i, peer in enumerate(xs)
    ]
    for i in range(1, 4):
        slot = lax.rem(x + i, 4)
        arrived(got.at[slot], recv_sem.at[slot])
    for copy in copies:
        copy.wait_send()
    top = jnp.maximum(
        jnp.maximum(got[0, 0], got[1, 0]), jnp.maximum(got[2, 0], got[3, 0])
    )
    total = jnp.zeros_like(top)
    for slot in range(4):
        total = total + got[slot, 1] * jnp.exp2(got[slot, 0] - top)
    out_ref[...] = top + jnp.log(total) * LOG2E


def combine(part):
    return pl.pallas_call(
        combine_kernel,
        out_shape=jax.ShapeDtypeStruct((8, LANES), F32),
        in_specs=[vmem_spec()],
        out_specs=vmem_spec(),
        scratch_shapes=[
            VMEM((4, 2, 8, LANES), F32),
            pltpu.SemaphoreType.DMA((3,)),
            pltpu.SemaphoreType.DMA((4,)),
        ],
        compiler_params=pltpu.CompilerParams(collective_id=1, has_side_effects=True),
        name="combine_totals",
    )(part)


def grads_kernel(
    meta_ref, qg_ref, gg_ref, kvg_ref, auxg_ref, segg_ref, log_ref,
    dq_ref, dkv_ref,
    ks, vs, kt, qt, gt, dqt, dk, dv,
):
    sort_keys(meta_ref, kvg_ref, 0, ks)
    sort_keys(meta_ref, kvg_ref, 1, vs)
    for b in range(KEYS // BLOCK):
        kt[b] = ks[pl.ds(b * BLOCK, BLOCK), :].T
    dk[...] = jnp.zeros_like(dk)
    dv[...] = jnp.zeros_like(dv)
    counts = key_counts(segg_ref)

    def span_step(s, carry):
        low, high, low_max, high_min, first, last = span_range(meta_ref, auxg_ref, counts, s)
        qt[...] = qg_ref[s].T
        gt[...] = gg_ref[s].T
        dqt[...] = jnp.zeros_like(dqt)
        log_total = log_ref[pl.ds(s, 1), :]
        delta = auxg_ref[s // 2, pl.ds(s % 2, 1), :]

        def tile(block, masked):
            rows = pl.ds(pl.multiple_of(block * BLOCK, BLOCK), BLOCK)
            scores = jnp.dot(ks[rows, :], qt[...], preferred_element_type=F32)
            probs = jnp.exp2(scores * (SCALE * LOG2E) - log_total)
            if masked:
                probs = jnp.where(inside(low, high, block), probs, 0.0)
            prob_grad = jnp.dot(vs[rows, :], gt[...], preferred_element_type=F32)
            score_grad = (SCALE * probs * (prob_grad - delta)).astype(BF16)
            dv[rows, :] += jnp.dot(probs.astype(BF16), gg_ref[s], preferred_element_type=F32)
            dk[rows, :] += jnp.dot(score_grad, qg_ref[s], preferred_element_type=F32)
            dqt[...] += jnp.dot(kt[block], score_grad, preferred_element_type=F32)

        def block_step(block, carry):
            edge = (block * BLOCK < low_max) | ((block + 1) * BLOCK > high_min)

            @pl.when(edge)
            def _():
                tile(block, True)

            @pl.when(jnp.logical_not(edge))
            def _():
                tile(block, False)

            return carry

        lax.fori_loop(first, last, block_step, 0)
        dq_ref[s] = dqt[...].T.astype(BF16)
        return carry

    lax.fori_loop(0, 8, span_step, 0)

    def unsort(t, carry):
        source = pl.ds(pl.multiple_of(meta_ref[t] * SPAN, SPAN), SPAN)
        target = pl.ds(pl.multiple_of((t % 2) * SPAN, SPAN), SPAN)
        dkv_ref[t // 2, target, pl.ds(0, DIM)] = dk[source, :].astype(BF16)
        dkv_ref[t // 2, target, pl.ds(DIM, DIM)] = dv[source, :].astype(BF16)
        return carry

    lax.fori_loop(0, 32, unsort, 0)


def grads(meta, qg, gg, kvg, auxg, segg, log_total):
    return pl.pallas_call(
        grads_kernel,
        out_shape=(
            jax.ShapeDtypeStruct((8, LANES, DIM), BF16),
            jax.ShapeDtypeStruct((16, ROWS, 2 * DIM), BF16),
        ),
        in_specs=[smem_spec()] + [vmem_spec()] * 6,
        out_specs=(vmem_spec(),) * 2,
        scratch_shapes=[
            VMEM((KEYS, DIM), BF16),
            VMEM((KEYS, DIM), BF16),
            VMEM((KEYS // BLOCK, DIM, BLOCK), BF16),
            VMEM((DIM, LANES), BF16),
            VMEM((DIM, LANES), BF16),
            VMEM((DIM, LANES), F32),
            VMEM((KEYS, DIM), F32),
            VMEM((KEYS, DIM), F32),
        ],
        compiler_params=pltpu.CompilerParams(vmem_limit_bytes=56 * 1024 * 1024),
        name="attention_grads",
    )(meta, qg, gg, kvg, auxg, segg, log_total)


def tail_kernel(
    dkv_ref, dq_ref, act_ref, w_ref, m1_ref, m2_ref,
    qgrad_ref, kvgrad_ref, nw_ref, n1_ref, n2_ref, trust_ref,
    dkv_in, dq_in, act_in, kv_in, partial, g_in, a_in, a_msg, b_in, b_msg,
    r_send, r_recv, x_send, x_recv, act_send, act_recv, kv_send, kv_recv,
    g_send, g_recv, a_send, a_recv, b_send, b_recv, own_sem,
):
    me, dp, x, rest = place()
    y_lo, z = rest // 8, rest % 8
    y_hi, core = dp // 2, dp % 2
    column = x * 4 + y_lo * 2 + y_hi
    line = z * 2 + core
    xs = x_peers(me, dp, x, rest)
    rs = rest_peers(me, dp, x, rest)

    def in_column(index):
        return ((index // 4) * 16 + (index // 2 % 2) * 8 + z, (index % 2) * 2 + core)

    def in_line(index):
        return (x * 16 + y_lo * 8 + index // 2, y_hi * 2 + index % 2)

    columns = [in_column(lax.rem(column + i, 16)) for i in range(1, 16)]
    lines = [in_line(lax.rem(line + i, 16)) for i in range(1, 16)]
    greeted = [
        (x * 16 + y_lo * 8 + lax.rem(z + i // 4, 8), lax.rem(dp + i % 4, 4)) for i in range(1, 32)
    ]
    greeted += [(x * 16 + (1 - y_lo) * 8 + i, dp) for i in range(8)]
    greeted += [
        (lax.rem(x + i, 4) * 16 + j * 8 + z, k * 2 + core)
        for i in range(1, 4) for j in range(2) for k in range(2)
    ]
    greeted += [(x * 16 + (1 - y_lo) * 8 + z, (1 - y_hi) * 2 + core)]
    barrier = greet(greeted)
    own = [
        pltpu.make_async_copy(dkv_ref.at[rest], dkv_in.at[rest], own_sem.at[0]),
        pltpu.make_async_copy(dq_ref.at[pl.ds(2 * x, 2)], dq_in.at[x], own_sem.at[1]),
        pltpu.make_async_copy(
            act_ref.at[:, pl.ds(pl.multiple_of(column * LANES, LANES), LANES)],
            act_in.at[0], own_sem.at[2],
        ),
    ]
    for copy in own:
        copy.start()
    pl.semaphore_wait(barrier, len(greeted))

    copies = []
    for i, peer in enumerate(rs):
        there = lax.rem(rest + i + 1, 16)
        copies.append(
            send(dkv_ref.at[there], dkv_in.at[rest], r_send.at[i], r_recv.at[rest], peer)
        )
    for i, peer in enumerate(xs):
        there = lax.rem(x + i + 1, 4)
        copies.append(
            send(dq_ref.at[pl.ds(2 * there, 2)], dq_in.at[x], x_send.at[i], x_recv.at[x], peer)
        )
    for i, peer in enumerate(columns):
        there = lax.rem(column + i + 1, 16)
        piece = act_ref.at[:, pl.ds(pl.multiple_of(there * LANES, LANES), LANES)]
        copies.append(
            send(piece, act_in.at[i + 1], act_send.at[i], act_recv.at[i], peer)
        )

    for copy in own:
        copy.wait()
    for i in range(1, 16):
        slot = lax.rem(rest + i, 16)
        arrived(dkv_in.at[slot], r_recv.at[slot])
    kv_sum = dkv_in[0].astype(F32)
    for slot in range(1, 16):
        kv_sum = kv_sum + dkv_in[slot].astype(F32)
    kv_low = kv_sum.astype(BF16)
    kv_in[0] = kv_low
    kvgrad_ref[...] = kv_low
    for i, peer in enumerate(columns):
        copies.append(send(kv_in.at[0], kv_in.at[i + 1], kv_send.at[i], kv_recv.at[i], peer))

    for i in range(1, 4):
        slot = lax.rem(x + i, 4)
        arrived(dq_in.at[slot], x_recv.at[slot])
    for span in range(2):
        for h in range(HEADS):
            rows = pl.ds(h * SPAN, SPAN)
            summed = dq_in[0, span, rows, :].astype(F32)
            for slot in range(1, 4):
                summed = summed + dq_in[slot, span, rows, :].astype(F32)
            qgrad_ref[pl.ds(span * SPAN, SPAN), pl.ds(h * DIM, DIM)] = summed.astype(BF16)

    total = jnp.zeros((2 * DIM, LANES), F32)
    for i in range(16):
        if i > 0:
            arrived(act_in.at[i], act_recv.at[i - 1])
            arrived(kv_in.at[i], kv_recv.at[i - 1])
        total = total + jnp.dot(kv_in[i].T, act_in[i], preferred_element_type=F32)
    partial[...] = total.T

    here = z // 4 == y_hi

    def owner(i):
        there_z = lax.rem(z % 4 + i // 4, 4)
        there_dp = lax.rem(dp + i % 4, 4)
        rows = pl.ds(pl.multiple_of((there_z * 4 + there_dp) * 32, 32), 32)
        return partial.at[rows], (x * 16 + y_lo * 8 + y_hi * 4 + there_z, there_dp)

    def to_owner(i):
        source, peer = owner(i)
        return pltpu.make_async_remote_copy(
            src_ref=source, dst_ref=g_in.at[line], send_sem=g_send.at[i],
            recv_sem=g_recv.at[line], device_id=peer, device_id_type=MESH,
        )

    for i in range(1, 16):
        to_owner(i).start()

    @pl.when(here)
    def _():
        pltpu.make_async_copy(owner(0)[0], g_in.at[line], g_recv.at[line]).start()

    @pl.when(jnp.logical_not(here))
    def _():
        to_owner(0).start()

    for slot in range(16):
        arrived(g_in.at[slot], g_recv.at[slot])
    gradient = g_in[0]
    for slot in range(1, 16):
        gradient = gradient + g_in[slot]

    sums, updates = [], []
    for p in range(2):
        grad = gradient[:, p * DIM:(p + 1) * DIM]
        weight = w_ref[p]
        one = beta_one * m1_ref[p] + (1.0 - beta_one) * grad
        two = beta_two * m2_ref[p] + (1.0 - beta_two) * grad * grad
        n1_ref[p] = one
        n2_ref[p] = two
        update = one / (jnp.sqrt(two) + epsilon) + weight_decay * weight
        updates.append(update)
        sums.append(jnp.sum(weight * weight, axis=0, keepdims=True))
        sums.append(jnp.sum(update * update, axis=0, keepdims=True))
    a_msg[...] = jnp.concatenate(sums + [jnp.zeros((4, DIM), F32)], axis=0)
    a_in[column] = a_msg[...]
    for i, peer in enumerate(columns):
        copies.append(send(a_msg, a_in.at[column], a_send.at[i], a_recv.at[column], peer))
    for i in range(1, 16):
        slot = lax.rem(column + i, 16)
        arrived(a_in.at[slot], a_recv.at[slot])
    summed = a_in[0]
    for slot in range(1, 16):
        summed = summed + a_in[slot]
    b_msg[...] = summed
    b_in[line] = summed
    for i, peer in enumerate(lines):
        copies.append(send(b_msg, b_in.at[line], b_send.at[i], b_recv.at[line], peer))
    for i in range(1, 16):
        slot = lax.rem(line + i, 16)
        arrived(b_in.at[slot], b_recv.at[slot])
    summed = b_in[0]
    for slot in range(1, 16):
        summed = summed + b_in[slot]
    norms = jnp.sqrt(jnp.sum(summed, axis=1, keepdims=True))
    ratios = []
    for p in range(2):
        ratio = norms[2 * p:2 * p + 1] / (norms[2 * p + 1:2 * p + 2] + epsilon)
        ratios.append(ratio)
        nw_ref[p] = w_ref[p] - learn_rate * ratio * updates[p]
    trust_ref[...] = jnp.concatenate(
        [jnp.broadcast_to(ratio, (1, DIM)) for ratio in ratios] + [jnp.zeros((6, DIM), F32)], axis=0
    )
    for copy in copies:
        copy.wait_send()
    for i in range(1, 16):
        to_owner(i).wait_send()

    @pl.when(jnp.logical_not(here))
    def _():
        to_owner(0).wait_send()


def tail(dkv, dq, act, kv_weight, moment_one, moment_two):
    state = jax.ShapeDtypeStruct((2, 32, DIM), F32)
    dma = pltpu.SemaphoreType.DMA
    return pl.pallas_call(
        tail_kernel,
        out_shape=(
            jax.ShapeDtypeStruct((ROWS, HEADS * DIM), BF16),
            jax.ShapeDtypeStruct((ROWS, 2 * DIM), BF16),
            state, state, state,
            jax.ShapeDtypeStruct((8, DIM), F32),
        ),
        in_specs=[any_spec()] * 3 + [vmem_spec()] * 3,
        out_specs=(vmem_spec(),) * 6,
        scratch_shapes=[
            VMEM((16, ROWS, 2 * DIM), BF16),
            VMEM((4, 2, LANES, DIM), BF16),
            VMEM((16, ROWS, LANES), BF16),
            VMEM((16, ROWS, 2 * DIM), BF16),
            VMEM((LANES, 2 * DIM), F32),
            VMEM((16, 32, 2 * DIM), F32),
            VMEM((16, 8, DIM), F32),
            VMEM((8, DIM), F32),
            VMEM((16, 8, DIM), F32),
            VMEM((8, DIM), F32),
            dma((15,)), dma((16,)),
            dma((3,)), dma((4,)),
            dma((15,)), dma((15,)),
            dma((15,)), dma((15,)),
            dma((16,)), dma((16,)),
            dma((15,)), dma((16,)),
            dma((15,)), dma((16,)),
            dma((3,)),
        ],
        compiler_params=pltpu.CompilerParams(
            collective_id=2, has_side_effects=True, vmem_limit_bytes=48 * 1024 * 1024
        ),
        name="reduce_and_update",
    )(dkv, dq, act, kv_weight, moment_one, moment_two)


def on_device(
    queries,
    key_states,
    value_states,
    attn_out,
    out_grad,
    activations,
    segment_ids,
    span_order,
    kv_weight,
    moment_one,
    moment_two,
):
    me = lax.axis_index("context")
    x, rest = me // 16, me % 16
    local = lax.dynamic_slice_in_dim(span_order, x * 32, 32, 0)
    mine = lax.dynamic_slice_in_dim(span_order.reshape(4, 16, 2), rest, 1, 1).reshape(8)
    asked = jnp.concatenate([local, mine])
    meta = jnp.sum((local[None, :] < asked[:, None]).astype(jnp.int32), axis=1)
    seg = segment_ids.astype(F32)
    seg_rows = jnp.tile(seg.reshape(2, 1, SPAN), (1, HEADS, 1)).reshape(2, LANES)
    seg_keys = jnp.broadcast_to(seg, (8, ROWS))
    qg, gg, kvg, auxg, segg = gather(
        queries[0], out_grad[0], attn_out[0], key_states[0], value_states[0], seg_rows, seg_keys
    )
    part = stats(meta, qg, kvg, auxg, segg)
    log_total = combine(part)
    dq, dkv = grads(meta, qg, gg, kvg, auxg, segg, log_total)
    query_grad, kv_grad, new_weight, new_one, new_two, trust = tail(
        dkv, dq, activations[0], kv_weight, moment_one, moment_two
    )
    return (query_grad[None], kv_grad[None], new_weight, new_one, new_two, trust[:2, 0])


def solution(mesh):
    in_specs = (
        P("dp", "context", None),
        P("dp", "context", None),
        P("dp", "context", None),
        P("dp", "context", None),
        P("dp", "context", None),
        P("dp", "context", None),
        P("dp", "context"),
        P(),
        P(None, ("context", "dp"), None),
        P(None, ("context", "dp"), None),
        P(None, ("context", "dp"), None),
    )
    out_specs = (
        P("dp", "context", None),
        P("dp", "context", None),
        P(None, ("context", "dp"), None),
        P(None, ("context", "dp"), None),
        P(None, ("context", "dp"), None),
        P(),
    )
    return jax.shard_map(
        on_device, mesh=mesh, in_specs=in_specs, out_specs=out_specs, check_vma=False
    )
```

```python
import functools

import jax
import jax.numpy as jnp
from jax import lax
from jax.experimental import pallas as pl
from jax.experimental.pallas import tpu as pltpu
from jax.sharding import PartitionSpec as P

beta_one = 0.9
beta_two = 0.999
epsilon = 1e-06
weight_decay = 0.01
learn_rate = 0.01

HEADS = 8
DIM = 128
SPAN = 64
ROWS = 128
LANES = HEADS * SPAN
BLOCK = 256
KEYS = 2048
EARLY = 8
SHIFTS = (1, 15, 2, 14, 3, 13, 4, 12, 5, 11, 6, 10, 7, 9, 8)
CHUNK = 512
VMEM_LIMIT = 62 * 1024 * 1024
SCALE = DIM ** (-0.5)
LOG2E = 1.4426950408889634
MESH = pl.DeviceIdType.MESH
VMEM = pltpu.VMEM
F32 = jnp.float32
BF16 = jnp.bfloat16


def vmem_spec():
    return pl.BlockSpec(memory_space=pltpu.VMEM)


def any_spec():
    return pl.BlockSpec(memory_space=pl.ANY)


def smem_spec():
    return pl.BlockSpec(memory_space=pltpu.SMEM)


def greet(peers):
    barrier = pltpu.get_barrier_semaphore()
    for peer in peers:
        pl.semaphore_signal(barrier, inc=1, device_id=peer, device_id_type=MESH)
    return barrier


def send(src, dst, send_sem, recv_sem, peer):
    copy = pltpu.make_async_remote_copy(
        src_ref=src, dst_ref=dst, send_sem=send_sem, recv_sem=recv_sem,
        device_id=peer, device_id_type=MESH,
    )
    copy.start()
    return copy


def arrived(dst, sem):
    pltpu.make_async_copy(dst, dst, sem).wait()


def place():
    me = lax.axis_index("context")
    dp = lax.axis_index("dp")
    return me, dp, me // 16, me % 16


def x_peers(me, dp, x, rest):
    return [(lax.rem(x + i, 4) * 16 + rest, dp) for i in range(1, 4)]


def rest_peers(me, dp, x, rest):
    return [(x * 16 + lax.rem(rest + i, 16), dp) for i in range(1, 16)]


def column_peers(me, dp):
    x, y_lo, z = me // 16, me // 8 % 2, me % 8
    y_hi, core = dp // 2, dp % 2
    column = x * 4 + y_lo * 2 + y_hi
    peers = []
    for shift in SHIFTS:
        there = lax.rem(column + shift, 16)
        peers.append(((there // 4) * 16 + (there // 2 % 2) * 8 + z, (there % 2) * 2 + core))
    return column, peers


def act_piece(act_ref, index):
    there = lax.rem(index, 16)
    return act_ref.at[:, pl.ds(pl.multiple_of(there * LANES, LANES), LANES)]


def gather_kernel(
    q_ref, g_ref, o_ref, k_ref, v_ref, act_ref, segk_ref, rows_ref, local_ref,
    qg_ref, kg_ref, auxg_ref, segg_ref, log_ref, gg_ref, vg_ref, actg_ref,
    q_own, g_own, o_own, gbuf, k_aug, q_aug, scores, part, got,
    x_send, x_recv, r_send, r_recv, act_send, act_recv, m_send, m_recv, own_sem,
):
    me, dp, x, rest = place()
    xs = x_peers(me, dp, x, rest)
    rs = rest_peers(me, dp, x, rest)
    column, columns = column_peers(me, dp)
    two = pl.ds(pl.multiple_of(2 * x, 2), 2)
    own = [
        pltpu.make_async_copy(k_ref, kg_ref.at[rest], own_sem.at[0]),
        pltpu.make_async_copy(segk_ref, segg_ref.at[rest], own_sem.at[1]),
        pltpu.make_async_copy(q_ref, q_own, own_sem.at[2]),
        pltpu.make_async_copy(g_ref, g_own, own_sem.at[3]),
        pltpu.make_async_copy(o_ref, o_own, own_sem.at[4]),
        pltpu.make_async_copy(v_ref, vg_ref.at[rest], own_sem.at[5]),
        pltpu.make_async_copy(rows_ref, auxg_ref.at[x], own_sem.at[6]),
    ]
    for copy in own:
        copy.start()
    barrier = greet(
        rs + [(lax.rem(me + i * 16, 64) // 16 * 16 + j * 8 + me % 8, k * 2 + dp % 2)
              for i in range(1, 4) for j in range(2) for k in range(2)]
        + [(x * 16 + j * 8 + me % 8, (1 - dp // 2) * 2 + dp % 2) for j in range(2)]
    )
    for copy in own:
        copy.wait()
    for span in range(2):
        rows = pl.ds(span * SPAN, SPAN)
        pieces = []
        for h in range(HEADS):
            cols = pl.ds(h * DIM, DIM)
            qg_ref[2 * x + span, pl.ds(h * SPAN, SPAN), :] = q_own[rows, cols]
            grad = g_own[rows, cols]
            gbuf[span, pl.ds(h * SPAN, SPAN), :] = grad
            pieces.append(grad.astype(F32) * o_own[rows, cols].astype(F32))
        product = jnp.concatenate(pieces, axis=0)
        auxg_ref[x, pl.ds(span, 1), :] = jnp.sum(product.T, axis=0, keepdims=True)
    pl.semaphore_wait(barrier, 15 + 12 + 2)

    copies = []
    for i, peer in enumerate(rs):
        if i < 3:
            copies.append(send(qg_ref.at[two], qg_ref.at[two], x_send.at[0, i], x_recv.at[0, x], xs[i]))
            copies.append(send(auxg_ref.at[x], auxg_ref.at[x], x_send.at[2, i], x_recv.at[2, x], xs[i]))
        copies.append(send(kg_ref.at[rest], kg_ref.at[rest], r_send.at[0, i], r_recv.at[0, rest], peer))
        copies.append(send(segk_ref, segg_ref.at[rest], r_send.at[1, i], r_recv.at[1, rest], peer))
    for i, peer in enumerate(rs):
        if i < 3:
            copies.append(send(gbuf, gg_ref.at[two], x_send.at[1, i], x_recv.at[1, x], xs[i]))
        copies.append(send(v_ref, vg_ref.at[rest], r_send.at[2, i], r_recv.at[2, rest], peer))
    own = pltpu.make_async_copy(gbuf, gg_ref.at[two], own_sem.at[3])
    own.start()
    for i in range(EARLY):
        copies.append(
            send(act_piece(act_ref, column + SHIFTS[i]), actg_ref.at[i], act_send.at[i],
                 act_recv.at[i], columns[i])
        )
    own.wait()

    for i in range(1, 16):
        slot = lax.rem(rest + i, 16)
        arrived(kg_ref.at[slot], r_recv.at[0, slot])
        arrived(segg_ref.at[slot], r_recv.at[1, slot])
    feature = lax.broadcasted_iota(jnp.int32, (DIM, ROWS), 0)
    half = lax.broadcasted_iota(jnp.int32, (DIM, ROWS), 1) // SPAN

    def key_step(slot, carry):
        seg = segg_ref[slot, pl.ds(0, 1), :].astype(jnp.int32)
        hot = (feature == seg) | (feature == 2 * slot + half + 4)
        rows = pl.ds(pl.multiple_of(slot * ROWS, ROWS), ROWS)
        k_aug[rows, pl.ds(0, DIM)] = kg_ref[slot]
        k_aug[rows, pl.ds(DIM, DIM)] = hot.astype(F32).T.astype(BF16)
        return carry

    lax.fori_loop(0, 16, key_step, 0)
    for i in range(1, 4):
        slot = lax.rem(x + i, 4)
        pair = pl.ds(2 * slot, 2)
        arrived(qg_ref.at[pair], x_recv.at[0, slot])
        arrived(auxg_ref.at[slot], x_recv.at[2, slot])

    document = lax.broadcasted_iota(jnp.int32, (DIM, LANES), 0)
    local = jnp.broadcast_to(local_ref[...], (DIM, LANES))

    def span_step(s, carry):
        slot = s // 2
        seg = auxg_ref[slot, pl.ds(2 + s % 2, 1), :].astype(jnp.int32)
        span = auxg_ref[slot, pl.ds(4 + s % 2, 1), :]
        unseen = ((document < 4) & (document != seg)) | (local > span)
        q_aug[pl.ds(0, DIM), :] = qg_ref[s].T
        q_aug[pl.ds(DIM, DIM), :] = jnp.where(unseen, -1e30, 0.0).astype(BF16)
        for c in range(0, KEYS, CHUNK):
            scores[pl.ds(c, CHUNK), :] = jnp.dot(
                k_aug[pl.ds(c, CHUNK), :], q_aug[...], preferred_element_type=F32
            )

        @pl.when(slot == x)
        def _():
            rows = pl.ds(pl.multiple_of(rest * ROWS + s % 2 * SPAN, SPAN), SPAN)
            later = lax.broadcasted_iota(jnp.int32, (SPAN, LANES), 0) > (
                lax.broadcasted_iota(jnp.int32, (SPAN, LANES), 1) % SPAN
            )
            scores[rows, :] = jnp.where(later, -1e30, scores[rows, :])

        top = jnp.max(scores[...], axis=0, keepdims=True)
        weights = jnp.exp2((scores[...] - top) * (SCALE * LOG2E))
        part[0, pl.ds(s, 1), :] = top
        part[1, pl.ds(s, 1), :] = jnp.sum(weights, axis=0, keepdims=True)
        return carry

    lax.fori_loop(0, 8, span_step, 0)
    got[x] = part[...]
    for i, peer in enumerate(xs):
        copies.append(send(part, got.at[x], m_send.at[i], m_recv.at[x], peer))
    for i in range(1, 4):
        slot = lax.rem(x + i, 4)
        arrived(got.at[slot], m_recv.at[slot])
    top = jnp.maximum(
        jnp.maximum(got[0, 0], got[1, 0]), jnp.maximum(got[2, 0], got[3, 0])
    )
    total = jnp.zeros_like(top)
    for slot in range(4):
        total = total + got[slot, 1] * jnp.exp2((got[slot, 0] - top) * (SCALE * LOG2E))
    log_ref[...] = top * (SCALE * LOG2E) + jnp.log(total) * LOG2E

    for i in range(1, 16):
        slot = lax.rem(rest + i, 16)
        arrived(vg_ref.at[slot], r_recv.at[2, slot])
    for i in range(1, 4):
        slot = lax.rem(x + i, 4)
        arrived(gg_ref.at[pl.ds(2 * slot, 2)], x_recv.at[1, slot])
    for i in range(EARLY):
        arrived(actg_ref.at[i], act_recv.at[i])
    for copy in copies:
        copy.wait_send()


def gather(queries, out_grad, attn_out, key_states, value_states, act, seg_keys, rows, local):
    dma = pltpu.SemaphoreType.DMA
    return pl.pallas_call(
        gather_kernel,
        out_shape=(
            jax.ShapeDtypeStruct((8, LANES, DIM), BF16),
            jax.ShapeDtypeStruct((16, ROWS, DIM), BF16),
            jax.ShapeDtypeStruct((4, 8, LANES), F32),
            jax.ShapeDtypeStruct((16, 8, ROWS), F32),
            jax.ShapeDtypeStruct((8, LANES), F32),
            jax.ShapeDtypeStruct((8, LANES, DIM), BF16),
            jax.ShapeDtypeStruct((16, ROWS, DIM), BF16),
            jax.ShapeDtypeStruct((EARLY, ROWS, LANES), BF16),
        ),
        in_specs=[any_spec()] * 8 + [vmem_spec()],
        out_specs=(vmem_spec(),) * 5 + (any_spec(),) * 3,
        scratch_shapes=[
            VMEM((ROWS, HEADS * DIM), BF16),
            VMEM((ROWS, HEADS * DIM), BF16),
            VMEM((ROWS, HEADS * DIM), BF16),
            VMEM((2, LANES, DIM), BF16),
            VMEM((KEYS, 2 * DIM), BF16),
            VMEM((2 * DIM, LANES), BF16),
            VMEM((KEYS, LANES), F32),
            VMEM((2, 8, LANES), F32),
            VMEM((4, 2, 8, LANES), F32),
            dma((3, 3)), dma((3, 4)),
            dma((3, 15)), dma((3, 16)),
            dma((EARLY,)), dma((EARLY,)),
            dma((3,)), dma((4,)),
            dma((7,)),
        ],
        compiler_params=pltpu.CompilerParams(
            collective_id=0, has_side_effects=True, vmem_limit_bytes=VMEM_LIMIT
        ),
        name="gather_and_totals",
    )(queries, out_grad, attn_out, key_states, value_states, act, seg_keys, rows, local)


def key_counts(segg_ref):
    seg = segg_ref[:, 0, :]
    return [jnp.sum((seg < d - 0.5).astype(F32)).astype(jnp.int32) for d in (1, 2, 3)]


def span_range(meta_ref, auxg_ref, counts, s):
    slot = s // 2
    seg = auxg_ref[slot, pl.ds(2 + s % 2, 1), :]
    low = jnp.where(
        seg > 2.5, counts[2], jnp.where(seg > 1.5, counts[1], jnp.where(seg > 0.5, counts[0], 0))
    )
    x = lax.axis_index("context") // 16
    own = (slot == x).astype(jnp.int32)
    base = meta_ref[32 + s] * SPAN
    row = lax.broadcasted_iota(jnp.int32, (1, LANES), 1) % SPAN
    high = base + own * (row + 1)
    low_min, low_max = jnp.min(low), jnp.max(low)
    high_min, high_max = base + own, base + own * SPAN
    first = low_min // BLOCK
    last = (high_max + BLOCK - 1) // BLOCK
    return low, high, low_max, high_min, first, last


def inside(low, high, block):
    place_of = block * BLOCK + lax.broadcasted_iota(jnp.int32, (BLOCK, LANES), 0)
    return (place_of >= low) & (place_of < high)


def sort_keys(meta_ref, stored_ref, sorted_ref):
    def step(t, carry):
        rank = meta_ref[t]
        source = pl.multiple_of((t % 2) * SPAN, SPAN)
        target = pl.multiple_of(rank * SPAN, SPAN)
        sorted_ref[pl.ds(target, SPAN), :] = stored_ref[t // 2, pl.ds(source, SPAN), :]
        return carry

    lax.fori_loop(0, 32, step, 0)


def grads_kernel(
    meta_ref, qg_ref, gg_ref, kg_ref, vg_ref, auxg_ref, segg_ref, log_ref,
    dq_ref, dkv_ref,
    ks, vs, kt, qt, gt, dqt, dk, dv,
):
    sort_keys(meta_ref, kg_ref, ks)
    sort_keys(meta_ref, vg_ref, vs)
    for b in range(KEYS // BLOCK):
        kt[b] = ks[pl.ds(b * BLOCK, BLOCK), :].T
    dk[...] = jnp.zeros_like(dk)
    dv[...] = jnp.zeros_like(dv)
    counts = key_counts(segg_ref)

    def span_step(s, carry):
        low, high, low_max, high_min, first, last = span_range(meta_ref, auxg_ref, counts, s)
        qt[...] = qg_ref[s].T
        gt[...] = gg_ref[s].T
        dqt[...] = jnp.zeros_like(dqt)
        log_total = log_ref[pl.ds(s, 1), :]
        delta = auxg_ref[s // 2, pl.ds(s % 2, 1), :]

        def tile(block, masked):
            rows = pl.ds(pl.multiple_of(block * BLOCK, BLOCK), BLOCK)
            scores = jnp.dot(ks[rows, :], qt[...], preferred_element_type=F32)
            probs = jnp.exp2(scores * (SCALE * LOG2E) - log_total)
            if masked:
                probs = jnp.where(inside(low, high, block), probs, 0.0)
            prob_grad = jnp.dot(vs[rows, :], gt[...], preferred_element_type=F32)
            score_grad = (SCALE * probs * (prob_grad - delta)).astype(BF16)
            dv[rows, :] += jnp.dot(probs.astype(BF16), gg_ref[s], preferred_element_type=F32)
            dk[rows, :] += jnp.dot(score_grad, qg_ref[s], preferred_element_type=F32)
            dqt[...] += jnp.dot(kt[block], score_grad, preferred_element_type=F32)

        def block_step(block, carry):
            edge = (block * BLOCK < low_max) | ((block + 1) * BLOCK > high_min)

            @pl.when(edge)
            def _():
                tile(block, True)

            @pl.when(jnp.logical_not(edge))
            def _():
                tile(block, False)

            return carry

        lax.fori_loop(first, last, block_step, 0)
        dq_ref[s] = dqt[...].T.astype(BF16)
        return carry

    lax.fori_loop(0, 8, span_step, 0)

    def unsort(t, carry):
        source = pl.ds(pl.multiple_of(meta_ref[t] * SPAN, SPAN), SPAN)
        target = pl.ds(pl.multiple_of((t % 2) * SPAN, SPAN), SPAN)
        dkv_ref[0, t // 2, target, :] = dk[source, :].astype(BF16)
        dkv_ref[1, t // 2, target, :] = dv[source, :].astype(BF16)
        return carry

    lax.fori_loop(0, 32, unsort, 0)


def grads(meta, qg, gg, kg, vg, auxg, segg, log_total):
    return pl.pallas_call(
        grads_kernel,
        out_shape=(
            jax.ShapeDtypeStruct((8, LANES, DIM), BF16),
            jax.ShapeDtypeStruct((2, 16, ROWS, DIM), BF16),
        ),
        in_specs=[smem_spec()] + [vmem_spec()] * 7,
        out_specs=(vmem_spec(),) * 2,
        scratch_shapes=[
            VMEM((KEYS, DIM), BF16),
            VMEM((KEYS, DIM), BF16),
            VMEM((KEYS // BLOCK, DIM, BLOCK), BF16),
            VMEM((DIM, LANES), BF16),
            VMEM((DIM, LANES), BF16),
            VMEM((DIM, LANES), F32),
            VMEM((KEYS, DIM), F32),
            VMEM((KEYS, DIM), F32),
        ],
        compiler_params=pltpu.CompilerParams(vmem_limit_bytes=VMEM_LIMIT),
        name="attention_grads",
    )(meta, qg, gg, kg, vg, auxg, segg, log_total)


def tail_kernel(
    dkv_ref, dq_ref, act_ref, actg_ref, w_ref, m1_ref, m2_ref,
    qgrad_ref, kvgrad_ref, nw_ref, n1_ref, n2_ref, trust_ref,
    dkv_in, dq_in, act_in, kv_in, partial, g_in, a_in, a_msg, b_in, b_msg,
    r_send, r_recv, x_send, x_recv, act_send, act_recv, kv_send, kv_recv,
    g_send, g_recv, a_send, a_recv, b_send, b_recv, own_sem,
):
    me, dp, x, rest = place()
    y_lo, z = rest // 8, rest % 8
    y_hi, core = dp // 2, dp % 2
    line = z * 2 + core
    xs = x_peers(me, dp, x, rest)
    rs = rest_peers(me, dp, x, rest)
    column, columns = column_peers(me, dp)

    def in_line(index):
        return (x * 16 + y_lo * 8 + index // 2, y_hi * 2 + index % 2)

    lines = [in_line(lax.rem(line + i, 16)) for i in range(1, 16)]
    greeted = [
        (x * 16 + y_lo * 8 + lax.rem(z + i // 4, 8), lax.rem(dp + i % 4, 4)) for i in range(1, 32)
    ]
    greeted += [(x * 16 + (1 - y_lo) * 8 + i, dp) for i in range(8)]
    greeted += [
        (lax.rem(x + i, 4) * 16 + j * 8 + z, k * 2 + core)
        for i in range(1, 4) for j in range(2) for k in range(2)
    ]
    greeted += [(x * 16 + (1 - y_lo) * 8 + z, (1 - y_hi) * 2 + core)]
    barrier = greet(greeted)
    own = [
        pltpu.make_async_copy(dkv_ref.at[:, rest], dkv_in.at[:, rest], own_sem.at[0]),
        pltpu.make_async_copy(dq_ref.at[pl.ds(2 * x, 2)], dq_in.at[x], own_sem.at[1]),
        pltpu.make_async_copy(act_piece(act_ref, column), act_in.at[0], own_sem.at[2]),
        pltpu.make_async_copy(actg_ref, act_in.at[pl.ds(1, EARLY)], own_sem.at[3]),
    ]
    for copy in own:
        copy.start()
    pl.semaphore_wait(barrier, len(greeted))

    copies = []
    for p in range(2):
        for i, peer in enumerate(rs):
            there = lax.rem(rest + i + 1, 16)
            copies.append(
                send(dkv_ref.at[p, there], dkv_in.at[p, rest], r_send.at[p, i],
                     r_recv.at[p, rest], peer)
            )
    for i in range(EARLY, 15):
        copies.append(
            send(act_piece(act_ref, column + SHIFTS[i]), act_in.at[i + 1], act_send.at[i],
                 act_recv.at[i], columns[i])
        )
    for copy in own:
        copy.wait()

    for p in range(2):
        for i in range(1, 16):
            slot = lax.rem(rest + i, 16)
            arrived(dkv_in.at[p, slot], r_recv.at[p, slot])
        summed = dkv_in[p, 0].astype(F32)
        for slot in range(1, 16):
            summed = summed + dkv_in[p, slot].astype(F32)
        kv_low = summed.astype(BF16)
        kv_in[p, 0] = kv_low
        kvgrad_ref[:, pl.ds(p * DIM, DIM)] = kv_low
        for i, peer in enumerate(columns):
            copies.append(
                send(kv_in.at[p, 0], kv_in.at[p, i + 1], kv_send.at[p, i], kv_recv.at[p, i], peer)
            )
    for i, peer in enumerate(xs):
        there = lax.rem(x + i + 1, 4)
        copies.append(
            send(dq_ref.at[pl.ds(2 * there, 2)], dq_in.at[x], x_send.at[i], x_recv.at[x], peer)
        )

    here = z // 4 == y_hi

    def to_owner(p, i):
        there_z = lax.rem(z % 4 + i // 4, 4)
        there_dp = lax.rem(dp + i % 4, 4)
        rows = pl.ds(pl.multiple_of((there_z * 4 + there_dp) * 32, 32), 32)
        return pltpu.make_async_remote_copy(
            src_ref=partial.at[p, rows], dst_ref=g_in.at[p, line], send_sem=g_send.at[p, i],
            recv_sem=g_recv.at[p, line],
            device_id=(x * 16 + y_lo * 8 + y_hi * 4 + there_z, there_dp), device_id_type=MESH,
        )

    own_rows = pl.ds(pl.multiple_of((z % 4 * 4 + dp) * 32, 32), 32)
    for i in range(EARLY, 15):
        arrived(act_in.at[i + 1], act_recv.at[i])
    for p in range(2):
        total = jnp.zeros((DIM, LANES), F32)
        for i in range(16):
            if i > 0:
                arrived(kv_in.at[p, i], kv_recv.at[p, i - 1])
            total = total + jnp.dot(kv_in[p, i].T, act_in[i], preferred_element_type=F32)
        partial[p] = total.T.astype(BF16)
        for i in range(1, 16):
            to_owner(p, i).start()

        @pl.when(here)
        def _():
            pltpu.make_async_copy(
                partial.at[p, own_rows], g_in.at[p, line], g_recv.at[p, line]
            ).start()

        @pl.when(jnp.logical_not(here))
        def _():
            to_owner(p, 0).start()

    sums, updates = [], []
    for p in range(2):
        for slot in range(16):
            arrived(g_in.at[p, slot], g_recv.at[p, slot])
        grad = g_in[p, 0].astype(F32)
        for slot in range(1, 16):
            grad = grad + g_in[p, slot].astype(F32)
        weight = w_ref[p]
        one = beta_one * m1_ref[p] + (1.0 - beta_one) * grad
        two = beta_two * m2_ref[p] + (1.0 - beta_two) * grad * grad
        n1_ref[p] = one
        n2_ref[p] = two
        update = one / (jnp.sqrt(two) + epsilon) + weight_decay * weight
        updates.append(update)
        sums.append(jnp.sum(weight * weight, axis=0, keepdims=True))
        sums.append(jnp.sum(update * update, axis=0, keepdims=True))
    a_msg[...] = jnp.concatenate(sums + [jnp.zeros((4, DIM), F32)], axis=0)
    a_in[column] = a_msg[...]
    for i, peer in enumerate(columns):
        copies.append(send(a_msg, a_in.at[column], a_send.at[i], a_recv.at[column], peer))

    for i in range(1, 4):
        slot = lax.rem(x + i, 4)
        arrived(dq_in.at[slot], x_recv.at[slot])
    for span in range(2):
        for h in range(HEADS):
            rows = pl.ds(h * SPAN, SPAN)
            summed = dq_in[0, span, rows, :].astype(F32)
            for slot in range(1, 4):
                summed = summed + dq_in[slot, span, rows, :].astype(F32)
            qgrad_ref[pl.ds(span * SPAN, SPAN), pl.ds(h * DIM, DIM)] = summed.astype(BF16)

    for i in range(1, 16):
        slot = lax.rem(column + i, 16)
        arrived(a_in.at[slot], a_recv.at[slot])
    summed = a_in[0]
    for slot in range(1, 16):
        summed = summed + a_in[slot]
    b_msg[...] = summed
    b_in[line] = summed
    late = [
        send(b_msg, b_in.at[line], b_send.at[i], b_recv.at[line], peer)
        for i, peer in enumerate(lines)
    ]
    for copy in copies:
        copy.wait_send()
    for p in range(2):
        for i in range(1, 16):
            to_owner(p, i).wait_send()

        @pl.when(jnp.logical_not(here))
        def _():
            to_owner(p, 0).wait_send()

    for i in range(1, 16):
        slot = lax.rem(line + i, 16)
        arrived(b_in.at[slot], b_recv.at[slot])
    summed = b_in[0]
    for slot in range(1, 16):
        summed = summed + b_in[slot]
    norms = jnp.sqrt(jnp.sum(summed, axis=1, keepdims=True))
    ratios = []
    for p in range(2):
        ratio = norms[2 * p:2 * p + 1] / (norms[2 * p + 1:2 * p + 2] + epsilon)
        ratios.append(ratio)
        nw_ref[p] = w_ref[p] - learn_rate * ratio * updates[p]
    trust_ref[...] = jnp.concatenate(
        [jnp.broadcast_to(ratio, (1, DIM)) for ratio in ratios] + [jnp.zeros((6, DIM), F32)], axis=0
    )
    for copy in late:
        copy.wait_send()


def tail(dkv, dq, act, actg, kv_weight, moment_one, moment_two):
    state = jax.ShapeDtypeStruct((2, 32, DIM), F32)
    dma = pltpu.SemaphoreType.DMA
    return pl.pallas_call(
        tail_kernel,
        out_shape=(
            jax.ShapeDtypeStruct((ROWS, HEADS * DIM), BF16),
            jax.ShapeDtypeStruct((ROWS, 2 * DIM), BF16),
            state, state, state,
            jax.ShapeDtypeStruct((8, DIM), F32),
        ),
        in_specs=[any_spec()] * 4 + [vmem_spec()] * 3,
        out_specs=(vmem_spec(),) * 6,
        scratch_shapes=[
            VMEM((2, 16, ROWS, DIM), BF16),
            VMEM((4, 2, LANES, DIM), BF16),
            VMEM((16, ROWS, LANES), BF16),
            VMEM((2, 16, ROWS, DIM), BF16),
            VMEM((2, LANES, DIM), BF16),
            VMEM((2, 16, 32, DIM), BF16),
            VMEM((16, 8, DIM), F32),
            VMEM((8, DIM), F32),
            VMEM((16, 8, DIM), F32),
            VMEM((8, DIM), F32),
            dma((2, 15)), dma((2, 16)),
            dma((3,)), dma((4,)),
            dma((15,)), dma((15,)),
            dma((2, 15)), dma((2, 15)),
            dma((2, 16)), dma((2, 16)),
            dma((15,)), dma((16,)),
            dma((15,)), dma((16,)),
            dma((4,)),
        ],
        compiler_params=pltpu.CompilerParams(
            collective_id=2, has_side_effects=True, vmem_limit_bytes=48 * 1024 * 1024
        ),
        name="reduce_and_update",
    )(dkv, dq, act, actg, kv_weight, moment_one, moment_two)


def on_device(
    queries,
    key_states,
    value_states,
    attn_out,
    out_grad,
    activations,
    segment_ids,
    span_order,
    kv_weight,
    moment_one,
    moment_two,
):
    me = lax.axis_index("context")
    x, rest = me // 16, me % 16
    local = lax.dynamic_slice_in_dim(span_order, x * 32, 32, 0)
    mine = lax.dynamic_slice_in_dim(span_order.reshape(4, 16, 2), rest, 1, 1).reshape(8)
    asked = jnp.concatenate([local, mine])
    meta = jnp.sum((local[None, :] < asked[:, None]).astype(jnp.int32), axis=1)
    seg = segment_ids.astype(F32).reshape(2, 1, SPAN)
    spans = lax.dynamic_slice_in_dim(span_order, 2 * me, 2, 0).astype(F32)
    rows = jnp.concatenate(
        [
            jnp.zeros((2, LANES), F32),
            jnp.tile(seg, (1, HEADS, 1)).reshape(2, LANES),
            jnp.broadcast_to(spans[:, None], (2, LANES)),
            jnp.zeros((2, LANES), F32),
        ]
    )
    seg_keys = jnp.broadcast_to(seg.reshape(1, ROWS), (8, ROWS))
    local_ids = jnp.pad(local.astype(F32), (4, DIM - 36), constant_values=-1.0)[:, None]
    qg, kg, auxg, segg, log_total, gg, vg, actg = gather(
        queries[0], out_grad[0], attn_out[0], key_states[0], value_states[0], activations[0],
        seg_keys, rows, local_ids,
    )
    dq, dkv = grads(meta, qg, gg, kg, vg, auxg, segg, log_total)
    query_grad, kv_grad, new_weight, new_one, new_two, trust = tail(
        dkv, dq, activations[0], actg, kv_weight, moment_one, moment_two
    )
    return (query_grad[None], kv_grad[None], new_weight, new_one, new_two, trust[:2, 0])


def solution(mesh):
    in_specs = (
        P("dp", "context", None),
        P("dp", "context", None),
        P("dp", "context", None),
        P("dp", "context", None),
        P("dp", "context", None),
        P("dp", "context", None),
        P("dp", "context"),
        P(),
        P(None, ("context", "dp"), None),
        P(None, ("context", "dp"), None),
        P(None, ("context", "dp"), None),
    )
    out_specs = (
        P("dp", "context", None),
        P("dp", "context", None),
        P(None, ("context", "dp"), None),
        P(None, ("context", "dp"), None),
        P(None, ("context", "dp"), None),
        P(),
    )
    return jax.shard_map(
        on_device, mesh=mesh, in_specs=in_specs, out_specs=out_specs, check_vma=False
    )
```

```python
import functools

import jax
import jax.numpy as jnp
from jax import lax
from jax.experimental import pallas as pl
from jax.experimental.pallas import tpu as pltpu
from jax.sharding import PartitionSpec as P

beta_one = 0.9
beta_two = 0.999
epsilon = 1e-06
weight_decay = 0.01
learn_rate = 0.01

HEADS = 8
DIM = 128
SPAN = 64
ROWS = 128
LANES = HEADS * SPAN
BLOCK = 256
KEYS = 2048
LOG_ROW = 48
SHIFTS = (1, 15, 2, 14, 3, 13, 4, 12, 5, 11, 6, 10, 7, 9, 8)
CHUNK = 512
VMEM_LIMIT = 62 * 1024 * 1024
SCALE = DIM ** (-0.5)
LOG2E = 1.4426950408889634
MESH = pl.DeviceIdType.MESH
VMEM = pltpu.VMEM
F32 = jnp.float32
BF16 = jnp.bfloat16


def vmem_spec():
    return pl.BlockSpec(memory_space=pltpu.VMEM)


def any_spec():
    return pl.BlockSpec(memory_space=pl.ANY)


def smem_spec():
    return pl.BlockSpec(memory_space=pltpu.SMEM)


def greet(peers):
    barrier = pltpu.get_barrier_semaphore()
    for peer in peers:
        pl.semaphore_signal(barrier, inc=1, device_id=peer, device_id_type=MESH)
    return barrier


def send(src, dst, send_sem, recv_sem, peer):
    copy = pltpu.make_async_remote_copy(
        src_ref=src, dst_ref=dst, send_sem=send_sem, recv_sem=recv_sem,
        device_id=peer, device_id_type=MESH,
    )
    copy.start()
    return copy


def arrived(dst, sem):
    pltpu.make_async_copy(dst, dst, sem).wait()


def place():
    me = lax.axis_index("context")
    dp = lax.axis_index("dp")
    return me, dp, me // 16, me % 16


def x_peers(me, dp, x, rest):
    return [(lax.rem(x + i, 4) * 16 + rest, dp) for i in range(1, 4)]


def rest_peers(me, dp, x, rest):
    return [(x * 16 + lax.rem(rest + i, 16), dp) for i in range(1, 16)]


def column_peers(me, dp):
    x, y_lo, z = me // 16, me // 8 % 2, me % 8
    y_hi, core = dp // 2, dp % 2
    column = x * 4 + y_lo * 2 + y_hi
    peers = []
    for shift in SHIFTS:
        there = lax.rem(column + shift, 16)
        peers.append(((there // 4) * 16 + (there // 2 % 2) * 8 + z, (there % 2) * 2 + core))
    return column, peers


def act_piece(act_ref, index):
    there = lax.rem(index, 16)
    return act_ref.at[:, pl.ds(pl.multiple_of(there * LANES, LANES), LANES)]


def pieces_of(value):
    first = value.astype(BF16)
    left = value - first.astype(F32)
    second = left.astype(BF16)
    third = (left - second.astype(F32)).astype(BF16)
    zeros = jnp.zeros((13, value.shape[1]), F32)
    return jnp.concatenate(
        [first.astype(F32), second.astype(F32), third.astype(F32), zeros], axis=0
    ).astype(BF16)


def whole_kernel(
    order_ref, q_ref, g_ref, o_ref, k_ref, v_ref, act_ref, seg_ref, w_ref, m1_ref, m2_ref,
    qgrad_ref, kvgrad_ref, update_ref, n1_ref, n2_ref, trust_ref,
    q_own, g_own, o_own, qg, gg, kg, vg, auxg, segg, k_aug, v_aug, q_aug, g_aug, kt,
    scores, part, got, dk_acc, dv_acc, dqt, dkv_out, dkv_in, dq_out, dq_in,
    act_in, kv_in, partial, g_in, a_in, a_msg, b_in, b_msg,
    x_send, x_recv, r_send, r_recv, act_send, act_recv, m_send, m_recv,
    d_send, d_recv, dq_send, dq_recv, kv_send, kv_recv,
    gr_send, gr_recv, a_send, a_recv, b_send, b_recv, own_sem,
):
    me, dp, x, rest = place()
    y_lo, z = rest // 8, rest % 8
    y_hi, core = dp // 2, dp % 2
    line = z * 2 + core
    xs = x_peers(me, dp, x, rest)
    rs = rest_peers(me, dp, x, rest)
    column, columns = column_peers(me, dp)
    two = pl.ds(pl.multiple_of(2 * x, 2), 2)

    def in_line(index):
        return (x * 16 + y_lo * 8 + index // 2, y_hi * 2 + index % 2)

    lines = [in_line(lax.rem(line + i, 16)) for i in range(1, 16)]
    own = [
        pltpu.make_async_copy(k_ref, kg.at[rest], own_sem.at[0]),
        pltpu.make_async_copy(q_ref, q_own, own_sem.at[2]),
        pltpu.make_async_copy(g_ref, g_own, own_sem.at[3]),
        pltpu.make_async_copy(o_ref, o_own, own_sem.at[4]),
        pltpu.make_async_copy(v_ref, vg.at[rest], own_sem.at[5]),
        pltpu.make_async_copy(act_piece(act_ref, column), act_in.at[0], own_sem.at[1]),
    ]
    for copy in own:
        copy.start()
    greeted = [
        (x * 16 + y_lo * 8 + lax.rem(z + i // 4, 8), lax.rem(dp + i % 4, 4)) for i in range(1, 32)
    ]
    greeted += [(x * 16 + (1 - y_lo) * 8 + i, dp) for i in range(8)]
    greeted += [
        (lax.rem(x + i, 4) * 16 + j * 8 + z, k * 2 + core)
        for i in range(1, 4) for j in range(2) for k in range(2)
    ]
    greeted += [(x * 16 + (1 - y_lo) * 8 + z, (1 - y_hi) * 2 + core)]
    barrier = greet(greeted)
    seg_own = jnp.broadcast_to(seg_ref[...], (8, ROWS)).astype(F32)
    segg[rest] = seg_own
    swapped = pltpu.roll(seg_own, SPAN, 1)
    lower = lax.broadcasted_iota(jnp.int32, (8, ROWS), 1) < SPAN
    row_of = lax.broadcasted_iota(jnp.int32, (8, LANES), 0)
    auxg[x] = jnp.where(
        row_of == 2, jnp.concatenate([jnp.where(lower, seg_own, swapped)] * 4, axis=1),
        jnp.where(
            row_of == 3, jnp.concatenate([jnp.where(lower, swapped, seg_own)] * 4, axis=1),
            jnp.where(row_of == 4, order_ref[2 * me], order_ref[2 * me + 1]).astype(F32),
        ),
    )
    span_row = lax.broadcasted_iota(jnp.int32, (DIM, DIM), 0)
    local = jnp.full((DIM, DIM), -1, jnp.int32)
    for t in range(32):
        local = jnp.where(span_row == t + 4, order_ref[32 * x + t], local)
    local = jnp.concatenate([local] * (LANES // DIM), axis=1).astype(F32)
    for copy in own:
        copy.wait()
    for span in range(2):
        rows = pl.ds(span * SPAN, SPAN)
        products = []
        for h in range(HEADS):
            cols = pl.ds(h * DIM, DIM)
            qg[2 * x + span, pl.ds(h * SPAN, SPAN), :] = q_own[rows, cols]
            grad = g_own[rows, cols]
            gg[2 * x + span, pl.ds(h * SPAN, SPAN), :] = grad
            products.append(grad.astype(F32) * o_own[rows, cols].astype(F32))
        product = jnp.concatenate(products, axis=0)
        auxg[x, pl.ds(span, 1), :] = jnp.sum(product.T, axis=0, keepdims=True)
    pl.semaphore_wait(barrier, len(greeted))

    copies = []
    for i, peer in enumerate(rs):
        if i < 3:
            copies.append(send(qg.at[two], qg.at[two], x_send.at[0, i], x_recv.at[0, x], xs[i]))
            copies.append(send(auxg.at[x], auxg.at[x], x_send.at[2, i], x_recv.at[2, x], xs[i]))
        copies.append(send(kg.at[rest], kg.at[rest], r_send.at[0, i], r_recv.at[0, rest], peer))
        copies.append(send(segg.at[rest], segg.at[rest], r_send.at[1, i], r_recv.at[1, rest], peer))
    for i, peer in enumerate(rs):
        if i < 3:
            copies.append(send(gg.at[two], gg.at[two], x_send.at[1, i], x_recv.at[1, x], xs[i]))
        copies.append(send(vg.at[rest], vg.at[rest], r_send.at[2, i], r_recv.at[2, rest], peer))
    for i in range(1, 16):
        slot = lax.rem(rest + i, 16)
        arrived(kg.at[slot], r_recv.at[0, slot])
        arrived(segg.at[slot], r_recv.at[1, slot])
    feature = lax.broadcasted_iota(jnp.int32, (DIM, ROWS), 0)
    half = lax.broadcasted_iota(jnp.int32, (DIM, ROWS), 1) // SPAN
    ones = (feature >= LOG_ROW) & (feature < LOG_ROW + 3)

    def key_step(slot, carry):
        seg = segg[slot, pl.ds(0, 1), :].astype(jnp.int32)
        hot = (feature == seg) | (feature == 2 * slot + half + 4) | ones
        rows = pl.ds(pl.multiple_of(slot * ROWS, ROWS), ROWS)
        k_aug[rows, pl.ds(0, DIM)] = kg[slot]
        k_aug[rows, pl.ds(DIM, DIM)] = hot.astype(F32).T.astype(BF16)
        return carry

    lax.fori_loop(0, 16, key_step, 0)
    for i in range(1, 4):
        slot = lax.rem(x + i, 4)
        pair = pl.ds(pl.multiple_of(2 * slot, 2), 2)
        arrived(qg.at[pair], x_recv.at[0, slot])
        arrived(auxg.at[slot], x_recv.at[2, slot])

    document = lax.broadcasted_iota(jnp.int32, (DIM, LANES), 0)

    def span_step(s, carry):
        slot = s // 2
        seg = auxg[slot, pl.ds(2 + s % 2, 1), :].astype(jnp.int32)
        span = auxg[slot, pl.ds(4 + s % 2, 1), :]
        unseen = ((document < 4) & (document != seg)) | (local > span)
        q_aug[s, pl.ds(0, DIM), :] = qg[s].T
        q_aug[s, pl.ds(DIM, DIM), :] = jnp.where(unseen, -1e30, 0.0).astype(BF16)

        @pl.when(slot == x)
        def _():
            for c in range(0, KEYS, CHUNK):
                scores[pl.ds(c, CHUNK), :] = jnp.dot(
                    k_aug[pl.ds(c, CHUNK), :], q_aug[s], preferred_element_type=F32
                )
            rows = pl.ds(pl.multiple_of(rest * ROWS + s % 2 * SPAN, SPAN), SPAN)
            later = lax.broadcasted_iota(jnp.int32, (SPAN, LANES), 0) > (
                lax.broadcasted_iota(jnp.int32, (SPAN, LANES), 1) % SPAN
            )
            scores[rows, :] = jnp.where(later, -1e30, scores[rows, :])
            top = jnp.max(scores[...], axis=0, keepdims=True)
            weights = jnp.exp2((scores[...] - top) * (SCALE * LOG2E))
            part[0, pl.ds(s, 1), :] = top
            part[1, pl.ds(s, 1), :] = jnp.sum(weights, axis=0, keepdims=True)

        @pl.when(slot != x)
        def _():
            top = jnp.full((8, LANES), -1e30, F32)
            total = jnp.zeros((8, LANES), F32)
            for c in range(0, KEYS, BLOCK):
                block = jnp.dot(
                    k_aug[pl.ds(c, BLOCK), :], q_aug[s], preferred_element_type=F32
                ).reshape(BLOCK // 8, 8, LANES)
                new = jnp.maximum(top, jnp.max(block, axis=0))
                weights = jnp.exp2((block - new) * (SCALE * LOG2E))
                total = total * jnp.exp2((top - new) * (SCALE * LOG2E)) + jnp.sum(weights, axis=0)
                top = new
            whole_top = jnp.max(top, axis=0, keepdims=True)
            total = total * jnp.exp2((top - whole_top) * (SCALE * LOG2E))
            part[0, pl.ds(s, 1), :] = whole_top
            part[1, pl.ds(s, 1), :] = jnp.sum(total, axis=0, keepdims=True)

        return carry

    lax.fori_loop(0, 8, span_step, 0)
    got[x] = part[...]
    for i, peer in enumerate(xs):
        copies.append(send(part, got.at[x], m_send.at[i], m_recv.at[x], peer))

    for i in range(1, 16):
        slot = lax.rem(rest + i, 16)
        arrived(vg.at[slot], r_recv.at[2, slot])
    for i in range(1, 4):
        slot = lax.rem(x + i, 4)
        arrived(gg.at[pl.ds(pl.multiple_of(2 * slot, 2), 2)], x_recv.at[1, slot])
    first_three = (lax.broadcasted_iota(jnp.int32, (ROWS, DIM), 1) < 3).astype(F32).astype(BF16)

    def value_step(slot, carry):
        rows = pl.ds(pl.multiple_of(slot * ROWS, ROWS), ROWS)
        v_aug[rows, pl.ds(0, DIM)] = vg[slot]
        v_aug[rows, pl.ds(DIM, DIM)] = first_three
        return carry

    lax.fori_loop(0, 16, value_step, 0)

    def turn_keys(b, carry):
        rows = pl.ds(pl.multiple_of(b * BLOCK, BLOCK), BLOCK)
        kt[b] = k_aug[rows, pl.ds(0, DIM)].T
        return carry

    lax.fori_loop(0, KEYS // BLOCK, turn_keys, 0)

    def grad_step(s, carry):
        g_aug[s, pl.ds(0, DIM), :] = gg[s].T
        g_aug[s, pl.ds(DIM, 16), :] = pieces_of(-auxg[s // 2, pl.ds(s % 2, 1), :])
        g_aug[s, pl.ds(DIM + 16, DIM - 16), :] = jnp.zeros((DIM - 16, LANES), BF16)
        dqt[s] = jnp.zeros((DIM, LANES), F32)
        return carry

    lax.fori_loop(0, 8, grad_step, 0)
    for i in range(1, 4):
        slot = lax.rem(x + i, 4)
        arrived(got.at[slot], m_recv.at[slot])
    top = jnp.maximum(
        jnp.maximum(got[0, 0], got[1, 0]), jnp.maximum(got[2, 0], got[3, 0])
    )
    total = jnp.zeros_like(top)
    for slot in range(4):
        total = total + got[slot, 1] * jnp.exp2((got[slot, 0] - top) * (SCALE * LOG2E))
    log_total = top + jnp.log(total) * (1.0 / SCALE)
    for s in range(8):
        q_aug[s, pl.ds(DIM + LOG_ROW, 16), :] = pieces_of(-log_total[s:s + 1])

    for i, peer in enumerate(columns):
        copies.append(
            send(act_piece(act_ref, column + SHIFTS[i]), act_in.at[i + 1], act_send.at[i],
                 act_recv.at[i], peer)
        )

    def tile(pair, s, masked):
        rows = pl.ds(pl.multiple_of(pair * BLOCK, BLOCK), BLOCK)
        probs = jnp.exp2(
            jnp.dot(k_aug[rows, :], q_aug[s], preferred_element_type=F32) * (SCALE * LOG2E)
        )
        if masked:
            key = lax.broadcasted_iota(jnp.int32, (BLOCK, LANES), 0) - (
                rest % 2 * ROWS + s % 2 * SPAN
            )
            key = jnp.where(s // 2 == x, key, SPAN)
            row = lax.broadcasted_iota(jnp.int32, (BLOCK, LANES), 1) % SPAN
            probs = jnp.where((key < SPAN) & (key > row), 0.0, probs)
        prob_grad = jnp.dot(v_aug[rows, :], g_aug[s], preferred_element_type=F32)
        score_grad = (probs * prob_grad * SCALE).astype(BF16)
        dv_acc[...] += jnp.dot(probs.astype(BF16), gg[s], preferred_element_type=F32)
        dk_acc[...] += jnp.dot(score_grad, qg[s], preferred_element_type=F32)
        dqt[s] += jnp.dot(kt[pair], score_grad, preferred_element_type=F32)

    def key_block(pair):
        dk_acc[...] = jnp.zeros_like(dk_acc)
        dv_acc[...] = jnp.zeros_like(dv_acc)

        def query_step(t, carry):
            diagonal = (t == x // 2) & (pair == rest // 2)

            @pl.when(diagonal)
            def _():
                for u in range(4):
                    tile(pair, 4 * t + u, True)

            @pl.when(jnp.logical_not(diagonal))
            def _():
                for u in range(4):
                    tile(pair, 4 * t + u, False)

            return carry

        lax.fori_loop(0, 2, query_step, 0)
        for h in range(2):
            dkv_out[2 * pair + h, 0] = dk_acc[pl.ds(h * ROWS, ROWS), :].astype(BF16)
            dkv_out[2 * pair + h, 1] = dv_acc[pl.ds(h * ROWS, ROWS), :].astype(BF16)

    def to_holder(b, h):
        slot = 2 * lax.rem(rest // 2 + 1 + b, 8) + h
        return pltpu.make_async_remote_copy(
            src_ref=dkv_out.at[slot], dst_ref=dkv_in.at[rest], send_sem=d_send.at[2 * b + h],
            recv_sem=d_recv.at[rest], device_id=(x * 16 + slot, dp), device_id_type=MESH,
        )

    def block_step(b, carry):
        key_block(lax.rem(rest // 2 + 1 + b, 8))
        to_holder(b, 0).start()
        to_holder(b, 1).start()
        return carry

    lax.fori_loop(0, 7, block_step, 0)
    key_block(rest // 2)
    other = rest + 1 - 2 * (rest % 2)
    copies.append(
        send(dkv_out.at[other], dkv_in.at[rest], d_send.at[14], d_recv.at[rest],
             (x * 16 + other, dp))
    )
    dkv_in[rest] = dkv_out[rest]

    def turn_queries(s, carry):
        dq_out[s] = dqt[s].T.astype(BF16)
        return carry

    lax.fori_loop(0, 8, turn_queries, 0)
    dq_in[x] = dq_out[two]

    for i in range(1, 16):
        slot = lax.rem(rest + i, 16)
        arrived(dkv_in.at[slot], d_recv.at[slot])
    for p in range(2):
        summed = dkv_in[0, p].astype(F32)
        for slot in range(1, 16):
            summed = summed + dkv_in[slot, p].astype(F32)
        kv_low = summed.astype(BF16)
        kv_in[p, 0] = kv_low
        kvgrad_ref[:, pl.ds(p * DIM, DIM)] = kv_low
        for i, peer in enumerate(columns):
            copies.append(
                send(kv_in.at[p, 0], kv_in.at[p, i + 1], kv_send.at[p, i], kv_recv.at[p, i], peer)
            )
    for i, peer in enumerate(xs):
        there = lax.rem(x + i + 1, 4)
        copies.append(
            send(dq_out.at[pl.ds(pl.multiple_of(2 * there, 2), 2)], dq_in.at[x], dq_send.at[i],
                 dq_recv.at[x], peer)
        )

    here = z // 4 == y_hi

    def to_owner(p, i):
        there_z = lax.rem(z % 4 + i // 4, 4)
        there_dp = lax.rem(dp + i % 4, 4)
        rows = pl.ds(pl.multiple_of((there_z * 4 + there_dp) * 32, 32), 32)
        return pltpu.make_async_remote_copy(
            src_ref=partial.at[p, rows], dst_ref=g_in.at[p, line], send_sem=gr_send.at[p, i],
            recv_sem=gr_recv.at[p, line],
            device_id=(x * 16 + y_lo * 8 + y_hi * 4 + there_z, there_dp), device_id_type=MESH,
        )

    own_rows = pl.ds(pl.multiple_of((z % 4 * 4 + dp) * 32, 32), 32)
    for i in range(15):
        arrived(act_in.at[i + 1], act_recv.at[i])
    for p in range(2):
        total = jnp.zeros((DIM, LANES), F32)
        for i in range(16):
            if i > 0:
                arrived(kv_in.at[p, i], kv_recv.at[p, i - 1])
            total = total + jnp.dot(kv_in[p, i].T, act_in[i], preferred_element_type=F32)
        partial[p] = total.T.astype(BF16)
        for i in range(1, 16):
            to_owner(p, i).start()

        @pl.when(here)
        def _():
            pltpu.make_async_copy(
                partial.at[p, own_rows], g_in.at[p, line], gr_recv.at[p, line]
            ).start()

        @pl.when(jnp.logical_not(here))
        def _():
            to_owner(p, 0).start()

    sums = []
    for p in range(2):
        for slot in range(16):
            arrived(g_in.at[p, slot], gr_recv.at[p, slot])
        grad = g_in[p, 0].astype(F32)
        for slot in range(1, 16):
            grad = grad + g_in[p, slot].astype(F32)
        weight = w_ref[p]
        one = beta_one * m1_ref[p] + (1.0 - beta_one) * grad
        two = beta_two * m2_ref[p] + (1.0 - beta_two) * grad * grad
        n1_ref[p] = one
        n2_ref[p] = two
        update = one / (jnp.sqrt(two) + epsilon) + weight_decay * weight
        update_ref[p] = update
        sums.append(jnp.sum(weight * weight, axis=0, keepdims=True))
        sums.append(jnp.sum(update * update, axis=0, keepdims=True))
    a_msg[...] = jnp.concatenate(sums + [jnp.zeros((4, DIM), F32)], axis=0)
    a_in[column] = a_msg[...]
    for i, peer in enumerate(columns):
        copies.append(send(a_msg, a_in.at[column], a_send.at[i], a_recv.at[column], peer))

    for i in range(1, 4):
        slot = lax.rem(x + i, 4)
        arrived(dq_in.at[slot], dq_recv.at[slot])
    for span in range(2):
        for h in range(HEADS):
            rows = pl.ds(h * SPAN, SPAN)
            summed = dq_in[0, span, rows, :].astype(F32)
            for slot in range(1, 4):
                summed = summed + dq_in[slot, span, rows, :].astype(F32)
            qgrad_ref[pl.ds(span * SPAN, SPAN), pl.ds(h * DIM, DIM)] = summed.astype(BF16)

    for i in range(1, 16):
        slot = lax.rem(column + i, 16)
        arrived(a_in.at[slot], a_recv.at[slot])
    summed = a_in[0]
    for slot in range(1, 16):
        summed = summed + a_in[slot]
    b_msg[...] = summed
    b_in[line] = summed
    late = [
        send(b_msg, b_in.at[line], b_send.at[i], b_recv.at[line], peer)
        for i, peer in enumerate(lines)
    ]
    for copy in copies:
        copy.wait_send()
    for b in range(7):
        to_holder(b, 0).wait_send()
        to_holder(b, 1).wait_send()
    for p in range(2):
        for i in range(1, 16):
            to_owner(p, i).wait_send()

        @pl.when(jnp.logical_not(here))
        def _():
            to_owner(p, 0).wait_send()

    for i in range(1, 16):
        slot = lax.rem(line + i, 16)
        arrived(b_in.at[slot], b_recv.at[slot])
    summed = b_in[0]
    for slot in range(1, 16):
        summed = summed + b_in[slot]
    norms = jnp.sqrt(jnp.sum(summed, axis=1, keepdims=True))
    ratios = []
    for p in range(2):
        ratio = norms[2 * p:2 * p + 1] / (norms[2 * p + 1:2 * p + 2] + epsilon)
        ratios.append(ratio)
    trust_ref[...] = jnp.concatenate(
        [jnp.broadcast_to(ratio, (1, DIM)) for ratio in ratios] + [jnp.zeros((6, DIM), F32)], axis=0
    )
    for copy in late:
        copy.wait_send()


def whole(span_order, queries, out_grad, attn_out, key_states, value_states, act, segment_ids,
          kv_weight, moment_one, moment_two):
    state = jax.ShapeDtypeStruct((2, 32, DIM), F32)
    dma = pltpu.SemaphoreType.DMA
    return pl.pallas_call(
        whole_kernel,
        out_shape=(
            jax.ShapeDtypeStruct((ROWS, HEADS * DIM), BF16),
            jax.ShapeDtypeStruct((ROWS, 2 * DIM), BF16),
            state, state, state,
            jax.ShapeDtypeStruct((8, DIM), F32),
        ),
        in_specs=[smem_spec()] + [any_spec()] * 6 + [vmem_spec()] * 4,
        out_specs=(vmem_spec(),) * 6,
        scratch_shapes=[
            VMEM((ROWS, HEADS * DIM), BF16),
            VMEM((ROWS, HEADS * DIM), BF16),
            VMEM((ROWS, HEADS * DIM), BF16),
            VMEM((8, LANES, DIM), BF16),
            VMEM((8, LANES, DIM), BF16),
            VMEM((16, ROWS, DIM), BF16),
            VMEM((16, ROWS, DIM), BF16),
            VMEM((4, 8, LANES), F32),
            VMEM((16, 8, ROWS), F32),
            VMEM((KEYS, 2 * DIM), BF16),
            VMEM((KEYS, 2 * DIM), BF16),
            VMEM((8, 2 * DIM, LANES), BF16),
            VMEM((8, 2 * DIM, LANES), BF16),
            VMEM((KEYS // BLOCK, DIM, BLOCK), BF16),
            VMEM((KEYS, LANES), F32),
            VMEM((2, 8, LANES), F32),
            VMEM((4, 2, 8, LANES), F32),
            VMEM((BLOCK, DIM), F32),
            VMEM((BLOCK, DIM), F32),
            VMEM((8, DIM, LANES), F32),
            VMEM((16, 2, ROWS, DIM), BF16),
            VMEM((16, 2, ROWS, DIM), BF16),
            VMEM((8, LANES, DIM), BF16),
            VMEM((4, 2, LANES, DIM), BF16),
            VMEM((16, ROWS, LANES), BF16),
            VMEM((2, 16, ROWS, DIM), BF16),
            VMEM((2, LANES, DIM), BF16),
            VMEM((2, 16, 32, DIM), BF16),
            VMEM((16, 8, DIM), F32),
            VMEM((8, DIM), F32),
            VMEM((16, 8, DIM), F32),
            VMEM((8, DIM), F32),
            dma((3, 3)), dma((3, 4)),
            dma((3, 15)), dma((3, 16)),
            dma((15,)), dma((15,)),
            dma((3,)), dma((4,)),
            dma((15,)), dma((16,)),
            dma((3,)), dma((4,)),
            dma((2, 15)), dma((2, 15)),
            dma((2, 16)), dma((2, 16)),
            dma((15,)), dma((16,)),
            dma((15,)), dma((16,)),
            dma((6,)),
        ],
        compiler_params=pltpu.CompilerParams(
            collective_id=0, has_side_effects=True, vmem_limit_bytes=VMEM_LIMIT
        ),
        name="attention_backward",
    )(span_order, queries, out_grad, attn_out, key_states, value_states, act, segment_ids,
      kv_weight, moment_one, moment_two)


def finish_kernel(
    q_ref, kv_ref, update_ref, one_ref, two_ref, ratio_ref, weight_ref,
    qgrad_ref, kvgrad_ref, nw_ref, n1_ref, n2_ref, trust_ref,
):
    qgrad_ref[0] = q_ref[...]
    kvgrad_ref[0] = kv_ref[...]
    n1_ref[...] = one_ref[...]
    n2_ref[...] = two_ref[...]
    for p in range(2):
        ratio = ratio_ref[pl.ds(p, 1), :]
        trust_ref[p] = ratio[0, 0]
        nw_ref[p] = weight_ref[p] - learn_rate * ratio * update_ref[p]


def finish(query_grad, kv_grad, update, new_one, new_two, ratio, kv_weight):
    state = jax.ShapeDtypeStruct((2, 32, DIM), F32)
    return pl.pallas_call(
        finish_kernel,
        out_shape=(
            jax.ShapeDtypeStruct((1, ROWS, HEADS * DIM), BF16),
            jax.ShapeDtypeStruct((1, ROWS, 2 * DIM), BF16),
            state, state, state,
            jax.ShapeDtypeStruct((2,), F32),
        ),
        in_specs=[vmem_spec()] * 7,
        out_specs=(vmem_spec(),) * 5 + (smem_spec(),),
        compiler_params=pltpu.CompilerParams(vmem_limit_bytes=VMEM_LIMIT),
        name="new_weights",
    )(query_grad, kv_grad, update, new_one, new_two, ratio, kv_weight)


def on_device(
    queries,
    key_states,
    value_states,
    attn_out,
    out_grad,
    activations,
    segment_ids,
    span_order,
    kv_weight,
    moment_one,
    moment_two,
):
    query_grad, kv_grad, update, new_one, new_two, trust = whole(
        span_order, queries[0], out_grad[0], attn_out[0], key_states[0], value_states[0],
        activations[0], segment_ids, kv_weight, moment_one, moment_two,
    )
    return finish(query_grad, kv_grad, update, new_one, new_two, trust, kv_weight)


def solution(mesh):
    in_specs = (
        P("dp", "context", None),
        P("dp", "context", None),
        P("dp", "context", None),
        P("dp", "context", None),
        P("dp", "context", None),
        P("dp", "context", None),
        P("dp", "context"),
        P(),
        P(None, ("context", "dp"), None),
        P(None, ("context", "dp"), None),
        P(None, ("context", "dp"), None),
    )
    out_specs = (
        P("dp", "context", None),
        P("dp", "context", None),
        P(None, ("context", "dp"), None),
        P(None, ("context", "dp"), None),
        P(None, ("context", "dp"), None),
        P(),
    )
    return jax.shard_map(
        on_device, mesh=mesh, in_specs=in_specs, out_specs=out_specs, check_vma=False
    )
```

```python
import functools

import jax
import jax.numpy as jnp
from jax import lax
from jax.experimental import pallas as pl
from jax.experimental.pallas import tpu as pltpu
from jax.sharding import PartitionSpec as P

beta_one = 0.9
beta_two = 0.999
epsilon = 1e-06
weight_decay = 0.01
learn_rate = 0.01

HEADS = 8
DIM = 128
SPAN = 64
ROWS = 128
LANES = HEADS * SPAN
BLOCK = 256
KEYS = 2048
LOG_ROW = 48
GROUP = 8
FEATURES = 1024
OWNERS = 32
SHIFTS = (1, 7, 2, 6, 3, 5, 4)
CHUNK = 512
VMEM_LIMIT = 62 * 1024 * 1024
SCALE = DIM ** (-0.5)
LOG2E = 1.4426950408889634
MESH = pl.DeviceIdType.MESH
VMEM = pltpu.VMEM
F32 = jnp.float32
BF16 = jnp.bfloat16


def vmem_spec():
    return pl.BlockSpec(memory_space=pltpu.VMEM)


def any_spec():
    return pl.BlockSpec(memory_space=pl.ANY)


def smem_spec():
    return pl.BlockSpec(memory_space=pltpu.SMEM)


def greet(peers):
    barrier = pltpu.get_barrier_semaphore()
    for peer in peers:
        pl.semaphore_signal(barrier, inc=1, device_id=peer, device_id_type=MESH)
    return barrier


def send(src, dst, send_sem, recv_sem, peer):
    copy = pltpu.make_async_remote_copy(
        src_ref=src, dst_ref=dst, send_sem=send_sem, recv_sem=recv_sem,
        device_id=peer, device_id_type=MESH,
    )
    copy.start()
    return copy


def arrived(dst, sem):
    pltpu.make_async_copy(dst, dst, sem).wait()


def place():
    me = lax.axis_index("context")
    dp = lax.axis_index("dp")
    return me, dp, me // 16, me % 16


def x_peers(me, dp, x, rest):
    return [(lax.rem(x + i, 4) * 16 + rest, dp) for i in range(1, 4)]


def rest_peers(me, dp, x, rest):
    return [(x * 16 + lax.rem(rest + i, 16), dp) for i in range(1, 16)]


def member_peers(me, dp):
    member = me // 16 * 2 + dp % 2
    peers = []
    for shift in SHIFTS:
        there = lax.rem(member + shift, GROUP)
        peers.append((there // 2 * 16 + me % 16, dp // 2 * 2 + there % 2))
    return member, peers


def act_piece(act_ref, index):
    there = lax.rem(index, GROUP)
    return act_ref.at[:, pl.ds(pl.multiple_of(there * FEATURES, FEATURES), FEATURES)]


def pieces_of(value):
    first = value.astype(BF16)
    left = value - first.astype(F32)
    second = left.astype(BF16)
    third = (left - second.astype(F32)).astype(BF16)
    zeros = jnp.zeros((13, value.shape[1]), F32)
    return jnp.concatenate(
        [first.astype(F32), second.astype(F32), third.astype(F32), zeros], axis=0
    ).astype(BF16)


def whole_kernel(
    order_ref, q_ref, g_ref, o_ref, k_ref, v_ref, act_ref, seg_ref, w_ref, m1_ref, m2_ref,
    qgrad_ref, kvgrad_ref, update_ref, n1_ref, n2_ref, trust_ref,
    q_own, g_own, o_own, qg, gg, kg, vg, auxg, delta, segg, k_aug, v_aug, q_aug, g_aug, kt,
    scores, part, got, dk_acc, dv_acc, dqt, dkv_out, dkv_in, dq_out, dq_in,
    act_in, kv_in, partial, g_in, a_in, a_msg, b_in, b_msg,
    x_send, x_recv, r_send, r_recv, act_send, act_recv, m_send, m_recv,
    d_send, d_recv, dq_send, dq_recv, kv_send, kv_recv,
    gr_send, gr_recv, a_send, a_recv, b_send, b_recv, own_sem,
):
    me, dp, x, rest = place()
    y_lo, z = rest // 8, rest % 8
    y_hi, core = dp // 2, dp % 2
    line = rest * 2 + y_hi
    xs = x_peers(me, dp, x, rest)
    rs = rest_peers(me, dp, x, rest)
    member, members = member_peers(me, dp)
    two = pl.ds(pl.multiple_of(2 * x, 2), 2)

    def in_line(index):
        return (x * 16 + index // 2, index % 2 * 2 + core)

    lines = [in_line(lax.rem(line + i, OWNERS)) for i in range(1, OWNERS)]
    own = [
        pltpu.make_async_copy(q_ref, q_own, own_sem.at[2]),
        pltpu.make_async_copy(k_ref, kg.at[rest], own_sem.at[0]),
        pltpu.make_async_copy(g_ref, g_own, own_sem.at[3]),
        pltpu.make_async_copy(o_ref, o_own, own_sem.at[4]),
        pltpu.make_async_copy(v_ref, vg.at[rest], own_sem.at[5]),
        pltpu.make_async_copy(act_piece(act_ref, member), act_in.at[0], own_sem.at[1]),
    ]
    for copy in own:
        copy.start()
    greeted = [
        (x * 16 + lax.rem(rest + i // 4, 16), lax.rem(dp + i % 4, 4)) for i in range(1, 64)
    ]
    greeted += [
        (lax.rem(x + i, 4) * 16 + rest, y_hi * 2 + j) for i in range(1, 4) for j in range(2)
    ]
    barrier = greet(greeted)
    seg_own = jnp.broadcast_to(seg_ref[...], (8, ROWS)).astype(F32)
    segg[rest] = seg_own
    swapped = pltpu.roll(seg_own, SPAN, 1)
    lower = lax.broadcasted_iota(jnp.int32, (8, ROWS), 1) < SPAN
    row_of = lax.broadcasted_iota(jnp.int32, (8, LANES), 0)
    auxg[x] = jnp.where(
        row_of == 0, jnp.concatenate([jnp.where(lower, seg_own, swapped)] * 4, axis=1),
        jnp.where(
            row_of == 1, jnp.concatenate([jnp.where(lower, swapped, seg_own)] * 4, axis=1),
            jnp.where(row_of == 2, order_ref[2 * me], order_ref[2 * me + 1]).astype(F32),
        ),
    )
    own[0].wait()
    own[1].wait()
    for span in range(2):
        for h in range(HEADS):
            qg[2 * x + span, pl.ds(h * SPAN, SPAN), :] = q_own[
                pl.ds(span * SPAN, SPAN), pl.ds(h * DIM, DIM)
            ]
    pl.semaphore_wait(barrier, len(greeted))

    copies = []
    for i, peer in enumerate(rs):
        if i < 3:
            copies.append(send(qg.at[two], qg.at[two], x_send.at[0, i], x_recv.at[0, x], xs[i]))
            copies.append(send(auxg.at[x], auxg.at[x], x_send.at[2, i], x_recv.at[2, x], xs[i]))
        copies.append(send(kg.at[rest], kg.at[rest], r_send.at[0, i], r_recv.at[0, rest], peer))
        copies.append(send(segg.at[rest], segg.at[rest], r_send.at[1, i], r_recv.at[1, rest], peer))
    for copy in own[2:]:
        copy.wait()
    for span in range(2):
        for h in range(HEADS):
            gg[2 * x + span, pl.ds(h * SPAN, SPAN), :] = g_own[
                pl.ds(span * SPAN, SPAN), pl.ds(h * DIM, DIM)
            ]
    for i, peer in enumerate(rs):
        if i < 3:
            copies.append(send(gg.at[two], gg.at[two], x_send.at[1, i], x_recv.at[1, x], xs[i]))
        copies.append(send(vg.at[rest], vg.at[rest], r_send.at[2, i], r_recv.at[2, rest], peer))
    delta[x] = jnp.zeros((8, LANES), F32)
    for span in range(2):
        rows = pl.ds(span * SPAN, SPAN)
        products = []
        for h in range(HEADS):
            cols = pl.ds(h * DIM, DIM)
            products.append(g_own[rows, cols].astype(F32) * o_own[rows, cols].astype(F32))
        product = jnp.concatenate(products, axis=0)
        delta[x, pl.ds(span, 1), :] = jnp.sum(product.T, axis=0, keepdims=True)
    for i, peer in enumerate(xs):
        copies.append(send(delta.at[x], delta.at[x], x_send.at[3, i], x_recv.at[3, x], peer))
    span_row = lax.broadcasted_iota(jnp.int32, (DIM, DIM), 0)
    local = jnp.full((DIM, DIM), -1, jnp.int32)
    for t in range(32):
        local = jnp.where(span_row == t + 4, order_ref[32 * x + t], local)
    local = jnp.concatenate([local] * (LANES // DIM), axis=1).astype(F32)

    for i in range(1, 16):
        slot = lax.rem(rest + i, 16)
        arrived(kg.at[slot], r_recv.at[0, slot])
        arrived(segg.at[slot], r_recv.at[1, slot])
    feature = lax.broadcasted_iota(jnp.int32, (DIM, ROWS), 0)
    half = lax.broadcasted_iota(jnp.int32, (DIM, ROWS), 1) // SPAN
    ones = (feature >= LOG_ROW) & (feature < LOG_ROW + 3)

    def key_step(slot, carry):
        seg = segg[slot, pl.ds(0, 1), :].astype(jnp.int32)
        hot = (feature == seg) | (feature == 2 * slot + half + 4) | ones
        rows = pl.ds(pl.multiple_of(slot * ROWS, ROWS), ROWS)
        k_aug[rows, pl.ds(0, DIM)] = kg[slot]
        k_aug[rows, pl.ds(DIM, DIM)] = hot.astype(F32).T.astype(BF16)
        return carry

    lax.fori_loop(0, 16, key_step, 0)
    for i in range(1, 4):
        slot = lax.rem(x + i, 4)
        pair = pl.ds(pl.multiple_of(2 * slot, 2), 2)
        arrived(qg.at[pair], x_recv.at[0, slot])
        arrived(auxg.at[slot], x_recv.at[2, slot])

    document = lax.broadcasted_iota(jnp.int32, (DIM, LANES), 0)

    def span_step(s, carry):
        slot = s // 2
        seg = auxg[slot, pl.ds(s % 2, 1), :].astype(jnp.int32)
        span = auxg[slot, pl.ds(2 + s % 2, 1), :]
        unseen = ((document < 4) & (document != seg)) | (local > span)
        q_aug[s, pl.ds(0, DIM), :] = qg[s].T
        q_aug[s, pl.ds(DIM, DIM), :] = jnp.where(unseen, -1e30, 0.0).astype(BF16)

        @pl.when(slot == x)
        def _():
            for c in range(0, KEYS, CHUNK):
                scores[pl.ds(c, CHUNK), :] = jnp.dot(
                    k_aug[pl.ds(c, CHUNK), :], q_aug[s], preferred_element_type=F32
                )
            rows = pl.ds(pl.multiple_of(rest * ROWS + s % 2 * SPAN, SPAN), SPAN)
            later = lax.broadcasted_iota(jnp.int32, (SPAN, LANES), 0) > (
                lax.broadcasted_iota(jnp.int32, (SPAN, LANES), 1) % SPAN
            )
            scores[rows, :] = jnp.where(later, -1e30, scores[rows, :])
            top = jnp.max(scores[...], axis=0, keepdims=True)
            weights = jnp.exp2((scores[...] - top) * (SCALE * LOG2E))
            part[0, pl.ds(s, 1), :] = top
            part[1, pl.ds(s, 1), :] = jnp.sum(weights, axis=0, keepdims=True)

        @pl.when(slot != x)
        def _():
            top = jnp.full((8, LANES), -1e30, F32)
            total = jnp.zeros((8, LANES), F32)
            for c in range(0, KEYS, BLOCK):
                block = jnp.dot(
                    k_aug[pl.ds(c, BLOCK), :], q_aug[s], preferred_element_type=F32
                ).reshape(BLOCK // 8, 8, LANES)
                new = jnp.maximum(top, jnp.max(block, axis=0))
                weights = jnp.exp2((block - new) * (SCALE * LOG2E))
                total = total * jnp.exp2((top - new) * (SCALE * LOG2E)) + jnp.sum(weights, axis=0)
                top = new
            whole_top = jnp.max(top, axis=0, keepdims=True)
            total = total * jnp.exp2((top - whole_top) * (SCALE * LOG2E))
            part[0, pl.ds(s, 1), :] = whole_top
            part[1, pl.ds(s, 1), :] = jnp.sum(total, axis=0, keepdims=True)

        return carry

    lax.fori_loop(0, 8, span_step, 0)
    got[x] = part[...]
    for i, peer in enumerate(xs):
        copies.append(send(part, got.at[x], m_send.at[i], m_recv.at[x], peer))

    for i in range(1, 16):
        slot = lax.rem(rest + i, 16)
        arrived(vg.at[slot], r_recv.at[2, slot])
    for i in range(1, 4):
        slot = lax.rem(x + i, 4)
        arrived(gg.at[pl.ds(pl.multiple_of(2 * slot, 2), 2)], x_recv.at[1, slot])
        arrived(delta.at[slot], x_recv.at[3, slot])
    first_three = (lax.broadcasted_iota(jnp.int32, (ROWS, DIM), 1) < 3).astype(F32).astype(BF16)

    def value_step(slot, carry):
        rows = pl.ds(pl.multiple_of(slot * ROWS, ROWS), ROWS)
        v_aug[rows, pl.ds(0, DIM)] = vg[slot]
        v_aug[rows, pl.ds(DIM, DIM)] = first_three
        return carry

    lax.fori_loop(0, 16, value_step, 0)

    def turn_keys(b, carry):
        rows = pl.ds(pl.multiple_of(b * BLOCK, BLOCK), BLOCK)
        kt[b] = k_aug[rows, pl.ds(0, DIM)].T
        return carry

    lax.fori_loop(0, KEYS // BLOCK, turn_keys, 0)

    def grad_step(s, carry):
        g_aug[s, pl.ds(0, DIM), :] = gg[s].T
        g_aug[s, pl.ds(DIM, 16), :] = pieces_of(-delta[s // 2, pl.ds(s % 2, 1), :])
        g_aug[s, pl.ds(DIM + 16, DIM - 16), :] = jnp.zeros((DIM - 16, LANES), BF16)
        dqt[s] = jnp.zeros((DIM, LANES), F32)
        return carry

    lax.fori_loop(0, 8, grad_step, 0)
    for i in range(1, 4):
        slot = lax.rem(x + i, 4)
        arrived(got.at[slot], m_recv.at[slot])
    top = jnp.maximum(
        jnp.maximum(got[0, 0], got[1, 0]), jnp.maximum(got[2, 0], got[3, 0])
    )
    total = jnp.zeros_like(top)
    for slot in range(4):
        total = total + got[slot, 1] * jnp.exp2((got[slot, 0] - top) * (SCALE * LOG2E))
    log_total = top + jnp.log(total) * (1.0 / SCALE)
    for s in range(8):
        q_aug[s, pl.ds(DIM + LOG_ROW, 16), :] = pieces_of(-log_total[s:s + 1])

    for i, peer in enumerate(members):
        copies.append(
            send(act_piece(act_ref, member + SHIFTS[i]), act_in.at[i + 1], act_send.at[i],
                 act_recv.at[i], peer)
        )

    def tile(pair, s, masked):
        rows = pl.ds(pl.multiple_of(pair * BLOCK, BLOCK), BLOCK)
        probs = jnp.exp2(
            jnp.dot(k_aug[rows, :], q_aug[s], preferred_element_type=F32) * (SCALE * LOG2E)
        )
        if masked:
            key = lax.broadcasted_iota(jnp.int32, (BLOCK, LANES), 0) - (
                rest % 2 * ROWS + s % 2 * SPAN
            )
            key = jnp.where(s // 2 == x, key, SPAN)
            row = lax.broadcasted_iota(jnp.int32, (BLOCK, LANES), 1) % SPAN
            probs = jnp.where((key < SPAN) & (key > row), 0.0, probs)
        prob_grad = jnp.dot(v_aug[rows, :], g_aug[s], preferred_element_type=F32)
        score_grad = (probs * prob_grad * SCALE).astype(BF16)
        dv_acc[...] += jnp.dot(probs.astype(BF16), gg[s], preferred_element_type=F32)
        dk_acc[...] += jnp.dot(score_grad, qg[s], preferred_element_type=F32)
        dqt[s] += jnp.dot(kt[pair], score_grad, preferred_element_type=F32)

    def key_block(pair):
        dk_acc[...] = jnp.zeros_like(dk_acc)
        dv_acc[...] = jnp.zeros_like(dv_acc)

        def query_step(t, carry):
            diagonal = (t == x // 2) & (pair == rest // 2)

            @pl.when(diagonal)
            def _():
                for u in range(4):
                    tile(pair, 4 * t + u, True)

            @pl.when(jnp.logical_not(diagonal))
            def _():
                for u in range(4):
                    tile(pair, 4 * t + u, False)

            return carry

        lax.fori_loop(0, 2, query_step, 0)
        for h in range(2):
            dkv_out[2 * pair + h, 0] = dk_acc[pl.ds(h * ROWS, ROWS), :].astype(BF16)
            dkv_out[2 * pair + h, 1] = dv_acc[pl.ds(h * ROWS, ROWS), :].astype(BF16)

    def to_holder(b, h):
        slot = 2 * lax.rem(rest // 2 + 1 + b, 8) + h
        return pltpu.make_async_remote_copy(
            src_ref=dkv_out.at[slot], dst_ref=dkv_in.at[rest], send_sem=d_send.at[2 * b + h],
            recv_sem=d_recv.at[rest], device_id=(x * 16 + slot, dp), device_id_type=MESH,
        )

    def block_step(b, carry):
        key_block(lax.rem(rest // 2 + 1 + b, 8))
        to_holder(b, 0).start()
        to_holder(b, 1).start()
        return carry

    lax.fori_loop(0, 7, block_step, 0)
    key_block(rest // 2)
    other = rest + 1 - 2 * (rest % 2)
    copies.append(
        send(dkv_out.at[other], dkv_in.at[rest], d_send.at[14], d_recv.at[rest],
             (x * 16 + other, dp))
    )
    dkv_in[rest] = dkv_out[rest]

    def turn_queries(s, carry):
        dq_out[s] = dqt[s].T.astype(BF16)
        return carry

    lax.fori_loop(0, 8, turn_queries, 0)
    dq_in[x] = dq_out[two]

    for i in range(1, 16):
        slot = lax.rem(rest + i, 16)
        arrived(dkv_in.at[slot], d_recv.at[slot])
    for p in range(2):
        summed = dkv_in[0, p].astype(F32)
        for slot in range(1, 16):
            summed = summed + dkv_in[slot, p].astype(F32)
        kv_low = summed.astype(BF16)
        kv_in[p, 0] = kv_low
        kvgrad_ref[:, pl.ds(p * DIM, DIM)] = kv_low
        for i, peer in enumerate(members):
            copies.append(
                send(kv_in.at[p, 0], kv_in.at[p, i + 1], kv_send.at[p, i], kv_recv.at[p, i], peer)
            )
    for i, peer in enumerate(xs):
        there = lax.rem(x + i + 1, 4)
        copies.append(
            send(dq_out.at[pl.ds(pl.multiple_of(2 * there, 2), 2)], dq_in.at[x], dq_send.at[i],
                 dq_recv.at[x], peer)
        )

    here = y_lo == core

    def to_owner(p, i):
        there_z = lax.rem(z + i // 4, 8)
        there_dp = lax.rem(dp + i % 4, 4)
        rows = pl.ds(pl.multiple_of((there_z * 4 + there_dp) * 32, 32), 32)
        return pltpu.make_async_remote_copy(
            src_ref=partial.at[p, rows], dst_ref=g_in.at[p, line], send_sem=gr_send.at[p, i],
            recv_sem=gr_recv.at[p, line],
            device_id=(x * 16 + core * 8 + there_z, there_dp), device_id_type=MESH,
        )

    own_rows = pl.ds(pl.multiple_of((z * 4 + dp) * 32, 32), 32)
    for i in range(GROUP - 1):
        arrived(act_in.at[i + 1], act_recv.at[i])
    for p in range(2):
        total = jnp.zeros((DIM, FEATURES), F32)
        for i in range(GROUP):
            if i > 0:
                arrived(kv_in.at[p, i], kv_recv.at[p, i - 1])
            total = total + jnp.dot(kv_in[p, i].T, act_in[i], preferred_element_type=F32)
        partial[p] = total.T.astype(BF16)
        for i in range(1, OWNERS):
            to_owner(p, i).start()

        @pl.when(here)
        def _():
            pltpu.make_async_copy(
                partial.at[p, own_rows], g_in.at[p, line], gr_recv.at[p, line]
            ).start()

        @pl.when(jnp.logical_not(here))
        def _():
            to_owner(p, 0).start()

    sums = []
    for p in range(2):
        for slot in range(OWNERS):
            arrived(g_in.at[p, slot], gr_recv.at[p, slot])
        grad = g_in[p, 0].astype(F32)
        for slot in range(1, OWNERS):
            grad = grad + g_in[p, slot].astype(F32)
        weight = w_ref[p]
        one = beta_one * m1_ref[p] + (1.0 - beta_one) * grad
        two = beta_two * m2_ref[p] + (1.0 - beta_two) * grad * grad
        n1_ref[p] = one
        n2_ref[p] = two
        update = one / (jnp.sqrt(two) + epsilon) + weight_decay * weight
        update_ref[p] = update
        sums.append(jnp.sum(weight * weight, axis=0, keepdims=True))
        sums.append(jnp.sum(update * update, axis=0, keepdims=True))
    a_msg[...] = jnp.concatenate(sums + [jnp.zeros((4, DIM), F32)], axis=0)
    a_in[member] = a_msg[...]
    for i, peer in enumerate(members):
        copies.append(send(a_msg, a_in.at[member], a_send.at[i], a_recv.at[member], peer))

    for i in range(1, GROUP):
        slot = lax.rem(member + i, GROUP)
        arrived(a_in.at[slot], a_recv.at[slot])
    summed = a_in[0]
    for slot in range(1, GROUP):
        summed = summed + a_in[slot]
    b_msg[...] = summed
    b_in[line] = summed
    late = [
        send(b_msg, b_in.at[line], b_send.at[i], b_recv.at[line], peer)
        for i, peer in enumerate(lines)
    ]
    for i in range(1, 4):
        slot = lax.rem(x + i, 4)
        arrived(dq_in.at[slot], dq_recv.at[slot])
    for span in range(2):
        for h in range(HEADS):
            rows = pl.ds(h * SPAN, SPAN)
            summed = dq_in[0, span, rows, :].astype(F32)
            for slot in range(1, 4):
                summed = summed + dq_in[slot, span, rows, :].astype(F32)
            qgrad_ref[pl.ds(span * SPAN, SPAN), pl.ds(h * DIM, DIM)] = summed.astype(BF16)

    for copy in copies:
        copy.wait_send()
    for b in range(7):
        to_holder(b, 0).wait_send()
        to_holder(b, 1).wait_send()
    for p in range(2):
        for i in range(1, OWNERS):
            to_owner(p, i).wait_send()

        @pl.when(jnp.logical_not(here))
        def _():
            to_owner(p, 0).wait_send()

    for i in range(1, OWNERS):
        slot = lax.rem(line + i, OWNERS)
        arrived(b_in.at[slot], b_recv.at[slot])
    summed = b_in[0]
    for slot in range(1, OWNERS):
        summed = summed + b_in[slot]
    norms = jnp.sqrt(jnp.sum(summed, axis=1, keepdims=True))
    ratios = []
    for p in range(2):
        ratio = norms[2 * p:2 * p + 1] / (norms[2 * p + 1:2 * p + 2] + epsilon)
        ratios.append(ratio)
    trust_ref[...] = jnp.concatenate(
        [jnp.broadcast_to(ratio, (1, DIM)) for ratio in ratios] + [jnp.zeros((6, DIM), F32)], axis=0
    )
    for copy in late:
        copy.wait_send()


def whole(span_order, queries, out_grad, attn_out, key_states, value_states, act, segment_ids,
          kv_weight, moment_one, moment_two):
    state = jax.ShapeDtypeStruct((2, 32, DIM), F32)
    dma = pltpu.SemaphoreType.DMA
    return pl.pallas_call(
        whole_kernel,
        out_shape=(
            jax.ShapeDtypeStruct((ROWS, HEADS * DIM), BF16),
            jax.ShapeDtypeStruct((ROWS, 2 * DIM), BF16),
            state, state, state,
            jax.ShapeDtypeStruct((8, DIM), F32),
        ),
        in_specs=[smem_spec()] + [any_spec()] * 6 + [vmem_spec()] * 4,
        out_specs=(vmem_spec(),) * 6,
        scratch_shapes=[
            VMEM((ROWS, HEADS * DIM), BF16),
            VMEM((ROWS, HEADS * DIM), BF16),
            VMEM((ROWS, HEADS * DIM), BF16),
            VMEM((8, LANES, DIM), BF16),
            VMEM((8, LANES, DIM), BF16),
            VMEM((16, ROWS, DIM), BF16),
            VMEM((16, ROWS, DIM), BF16),
            VMEM((4, 8, LANES), F32),
            VMEM((4, 8, LANES), F32),
            VMEM((16, 8, ROWS), F32),
            VMEM((KEYS, 2 * DIM), BF16),
            VMEM((KEYS, 2 * DIM), BF16),
            VMEM((8, 2 * DIM, LANES), BF16),
            VMEM((8, 2 * DIM, LANES), BF16),
            VMEM((KEYS // BLOCK, DIM, BLOCK), BF16),
            VMEM((KEYS, LANES), F32),
            VMEM((2, 8, LANES), F32),
            VMEM((4, 2, 8, LANES), F32),
            VMEM((BLOCK, DIM), F32),
            VMEM((BLOCK, DIM), F32),
            VMEM((8, DIM, LANES), F32),
            VMEM((16, 2, ROWS, DIM), BF16),
            VMEM((16, 2, ROWS, DIM), BF16),
            VMEM((8, LANES, DIM), BF16),
            VMEM((4, 2, LANES, DIM), BF16),
            VMEM((GROUP, ROWS, FEATURES), BF16),
            VMEM((2, GROUP, ROWS, DIM), BF16),
            VMEM((2, FEATURES, DIM), BF16),
            VMEM((2, OWNERS, 32, DIM), BF16),
            VMEM((GROUP, 8, DIM), F32),
            VMEM((8, DIM), F32),
            VMEM((OWNERS, 8, DIM), F32),
            VMEM((8, DIM), F32),
            dma((4, 3)), dma((4, 4)),
            dma((3, 15)), dma((3, 16)),
            dma((7,)), dma((7,)),
            dma((3,)), dma((4,)),
            dma((15,)), dma((16,)),
            dma((3,)), dma((4,)),
            dma((2, 7)), dma((2, 7)),
            dma((2, OWNERS)), dma((2, OWNERS)),
            dma((7,)), dma((GROUP,)),
            dma((31,)), dma((OWNERS,)),
            dma((6,)),
        ],
        compiler_params=pltpu.CompilerParams(
            collective_id=0, has_side_effects=True, vmem_limit_bytes=VMEM_LIMIT
        ),
        name="attention_backward",
    )(span_order, queries, out_grad, attn_out, key_states, value_states, act, segment_ids,
      kv_weight, moment_one, moment_two)


def finish_kernel(
    q_ref, kv_ref, update_ref, one_ref, two_ref, ratio_ref, weight_ref,
    qgrad_ref, kvgrad_ref, nw_ref, n1_ref, n2_ref, trust_ref,
):
    qgrad_ref[0] = q_ref[...]
    kvgrad_ref[0] = kv_ref[...]
    n1_ref[...] = one_ref[...]
    n2_ref[...] = two_ref[...]
    for p in range(2):
        ratio = ratio_ref[pl.ds(p, 1), :]
        trust_ref[p] = ratio[0, 0]
        nw_ref[p] = weight_ref[p] - learn_rate * ratio * update_ref[p]


def finish(query_grad, kv_grad, update, new_one, new_two, ratio, kv_weight):
    state = jax.ShapeDtypeStruct((2, 32, DIM), F32)
    return pl.pallas_call(
        finish_kernel,
        out_shape=(
            jax.ShapeDtypeStruct((1, ROWS, HEADS * DIM), BF16),
            jax.ShapeDtypeStruct((1, ROWS, 2 * DIM), BF16),
            state, state, state,
            jax.ShapeDtypeStruct((2,), F32),
        ),
        in_specs=[vmem_spec()] * 7,
        out_specs=(vmem_spec(),) * 5 + (smem_spec(),),
        compiler_params=pltpu.CompilerParams(vmem_limit_bytes=VMEM_LIMIT),
        name="new_weights",
    )(query_grad, kv_grad, update, new_one, new_two, ratio, kv_weight)


def on_device(
    queries,
    key_states,
    value_states,
    attn_out,
    out_grad,
    activations,
    segment_ids,
    span_order,
    kv_weight,
    moment_one,
    moment_two,
):
    query_grad, kv_grad, update, new_one, new_two, trust = whole(
        span_order, queries[0], out_grad[0], attn_out[0], key_states[0], value_states[0],
        activations[0], segment_ids, kv_weight, moment_one, moment_two,
    )
    return finish(query_grad, kv_grad, update, new_one, new_two, trust, kv_weight)


def solution(mesh):
    in_specs = (
        P("dp", "context", None),
        P("dp", "context", None),
        P("dp", "context", None),
        P("dp", "context", None),
        P("dp", "context", None),
        P("dp", "context", None),
        P("dp", "context"),
        P(),
        P(None, ("context", "dp"), None),
        P(None, ("context", "dp"), None),
        P(None, ("context", "dp"), None),
    )
    out_specs = (
        P("dp", "context", None),
        P("dp", "context", None),
        P(None, ("context", "dp"), None),
        P(None, ("context", "dp"), None),
        P(None, ("context", "dp"), None),
        P(),
    )
    return jax.shard_map(
        on_device, mesh=mesh, in_specs=in_specs, out_specs=out_specs, check_vma=False
    )
```

```python
import functools

import jax
import jax.numpy as jnp
from jax import lax
from jax.experimental import pallas as pl
from jax.experimental.pallas import tpu as pltpu
from jax.sharding import PartitionSpec as P

beta_one = 0.9
beta_two = 0.999
epsilon = 1e-06
weight_decay = 0.01
learn_rate = 0.01

HEADS = 8
DIM = 128
SPAN = 64
ROWS = 128
LANES = HEADS * SPAN
BLOCK = 256
KEYS = 2048
LOG_ROW = 48
GROUP = 8
FEATURES = 1024
OWNERS = 32
FAR_FIRST = sorted(
    range(1, OWNERS), key=lambda i: -min(i // 2 % 8, 8 - i // 2 % 8) - (0, 2, 1, 1)[i // 16 * 2 + i % 2]
)
SHIFTS = (1, 7, 2, 6, 3, 5, 4)
CHUNK = 512
VMEM_LIMIT = 62 * 1024 * 1024
SCALE = DIM ** (-0.5)
LOG2E = 1.4426950408889634
MESH = pl.DeviceIdType.MESH
VMEM = pltpu.VMEM
F32 = jnp.float32
BF16 = jnp.bfloat16


def vmem_spec():
    return pl.BlockSpec(memory_space=pltpu.VMEM)


def any_spec():
    return pl.BlockSpec(memory_space=pl.ANY)


def smem_spec():
    return pl.BlockSpec(memory_space=pltpu.SMEM)


def greet(peers):
    barrier = pltpu.get_barrier_semaphore()
    for peer in peers:
        pl.semaphore_signal(barrier, inc=1, device_id=peer, device_id_type=MESH)
    return barrier


def send(src, dst, send_sem, recv_sem, peer):
    copy = pltpu.make_async_remote_copy(
        src_ref=src, dst_ref=dst, send_sem=send_sem, recv_sem=recv_sem,
        device_id=peer, device_id_type=MESH,
    )
    copy.start()
    return copy


def arrived(dst, sem):
    pltpu.make_async_copy(dst, dst, sem).wait()


def place():
    me = lax.axis_index("context")
    dp = lax.axis_index("dp")
    return me, dp, me // 16, me % 16


def x_peers(me, dp, x, rest):
    return [(lax.rem(x + i, 4) * 16 + rest, dp) for i in range(1, 4)]


def rest_peers(me, dp, x, rest):
    return [(x * 16 + lax.rem(rest + i, 16), dp) for i in range(1, 16)]


def member_peers(me, dp):
    member = me // 16 * 2 + dp % 2
    peers = []
    for shift in SHIFTS:
        there = lax.rem(member + shift, GROUP)
        peers.append((there // 2 * 16 + me % 16, dp // 2 * 2 + there % 2))
    return member, peers


def act_piece(act_ref, index):
    there = lax.rem(index, GROUP)
    return act_ref.at[:, pl.ds(pl.multiple_of(there * FEATURES, FEATURES), FEATURES)]


def pieces_of(value):
    first = value.astype(BF16)
    left = value - first.astype(F32)
    second = left.astype(BF16)
    third = (left - second.astype(F32)).astype(BF16)
    zeros = jnp.zeros((13, value.shape[1]), F32)
    return jnp.concatenate(
        [first.astype(F32), second.astype(F32), third.astype(F32), zeros], axis=0
    ).astype(BF16)


def whole_kernel(
    order_ref, q_ref, g_ref, o_ref, k_ref, v_ref, act_ref, seg_ref, w_hbm, m1_hbm, m2_hbm,
    qgrad_ref, kvgrad_ref, update_ref, n1_ref, n2_ref, trust_ref,
    w_ref, m1_ref, m2_ref, q_own, g_own, o_own, qg, gg, kg, vg, auxg, delta, segg, k_aug, v_aug, q_aug, g_aug, kt,
    scores, part, got, dk_acc, dv_acc, dqt, dkv_out, dkv_in, dq_out, dq_in,
    act_in, kv_in, partial, g_in, a_in, a_msg, b_in, b_msg,
    x_send, x_recv, r_send, r_recv, act_send, act_recv, m_send, m_recv,
    d_send, d_recv, dq_send, dq_recv, kv_send, kv_recv,
    gr_send, gr_recv, a_send, a_recv, b_send, b_recv, own_sem,
):
    me, dp, x, rest = place()
    y_lo, z = rest // 8, rest % 8
    y_hi, core = dp // 2, dp % 2
    line = rest * 2 + y_hi
    xs = x_peers(me, dp, x, rest)
    rs = rest_peers(me, dp, x, rest)
    member, members = member_peers(me, dp)
    two = pl.ds(pl.multiple_of(2 * x, 2), 2)

    def in_line(index):
        return (x * 16 + index // 2, index % 2 * 2 + core)

    lines = [in_line(lax.rem(line + i, OWNERS)) for i in FAR_FIRST]
    own = [
        pltpu.make_async_copy(q_ref, q_own, own_sem.at[2]),
        pltpu.make_async_copy(k_ref, kg.at[rest], own_sem.at[0]),
        pltpu.make_async_copy(g_ref, g_own, own_sem.at[3]),
        pltpu.make_async_copy(o_ref, o_own, own_sem.at[4]),
        pltpu.make_async_copy(v_ref, vg.at[rest], own_sem.at[5]),
        pltpu.make_async_copy(act_piece(act_ref, member), act_in.at[0], own_sem.at[1]),
        pltpu.make_async_copy(w_hbm, w_ref, own_sem.at[6]),
        pltpu.make_async_copy(m1_hbm, m1_ref, own_sem.at[7]),
        pltpu.make_async_copy(m2_hbm, m2_ref, own_sem.at[8]),
    ]
    for copy in own:
        copy.start()
    greeted = [
        (x * 16 + lax.rem(rest + i // 4, 16), lax.rem(dp + i % 4, 4)) for i in range(1, 64)
    ]
    greeted += [
        (lax.rem(x + i, 4) * 16 + rest, y_hi * 2 + j) for i in range(1, 4) for j in range(2)
    ]
    barrier = greet(greeted)
    seg_own = jnp.broadcast_to(seg_ref[...], (8, ROWS)).astype(F32)
    segg[rest] = seg_own
    swapped = pltpu.roll(seg_own, SPAN, 1)
    lower = lax.broadcasted_iota(jnp.int32, (8, ROWS), 1) < SPAN
    row_of = lax.broadcasted_iota(jnp.int32, (8, LANES), 0)
    auxg[x] = jnp.where(
        row_of == 0, jnp.concatenate([jnp.where(lower, seg_own, swapped)] * 4, axis=1),
        jnp.where(
            row_of == 1, jnp.concatenate([jnp.where(lower, swapped, seg_own)] * 4, axis=1),
            jnp.where(row_of == 2, order_ref[2 * me], order_ref[2 * me + 1]).astype(F32),
        ),
    )
    own[0].wait()
    own[1].wait()
    for span in range(2):
        for h in range(HEADS):
            qg[2 * x + span, pl.ds(h * SPAN, SPAN), :] = q_own[
                pl.ds(span * SPAN, SPAN), pl.ds(h * DIM, DIM)
            ]
    pl.semaphore_wait(barrier, len(greeted))

    copies = []
    for i, peer in enumerate(rs):
        if i < 3:
            copies.append(send(qg.at[two], qg.at[two], x_send.at[0, i], x_recv.at[0, x], xs[i]))
            copies.append(send(auxg.at[x], auxg.at[x], x_send.at[2, i], x_recv.at[2, x], xs[i]))
        copies.append(send(kg.at[rest], kg.at[rest], r_send.at[0, i], r_recv.at[0, rest], peer))
        copies.append(send(segg.at[rest], segg.at[rest], r_send.at[1, i], r_recv.at[1, rest], peer))
    for copy in own[2:]:
        copy.wait()
    for span in range(2):
        for h in range(HEADS):
            gg[2 * x + span, pl.ds(h * SPAN, SPAN), :] = g_own[
                pl.ds(span * SPAN, SPAN), pl.ds(h * DIM, DIM)
            ]
    for i, peer in enumerate(rs):
        if i < 3:
            copies.append(send(gg.at[two], gg.at[two], x_send.at[1, i], x_recv.at[1, x], xs[i]))
        copies.append(send(vg.at[rest], vg.at[rest], r_send.at[2, i], r_recv.at[2, rest], peer))
    delta[x] = jnp.zeros((8, LANES), F32)
    for span in range(2):
        rows = pl.ds(span * SPAN, SPAN)
        products = []
        for h in range(HEADS):
            cols = pl.ds(h * DIM, DIM)
            products.append(g_own[rows, cols].astype(F32) * o_own[rows, cols].astype(F32))
        product = jnp.concatenate(products, axis=0)
        delta[x, pl.ds(span, 1), :] = jnp.sum(product.T, axis=0, keepdims=True)
    for i, peer in enumerate(xs):
        copies.append(send(delta.at[x], delta.at[x], x_send.at[3, i], x_recv.at[3, x], peer))
    span_row = lax.broadcasted_iota(jnp.int32, (DIM, DIM), 0)
    local = jnp.full((DIM, DIM), -1, jnp.int32)
    for t in range(32):
        local = jnp.where(span_row == t + 4, order_ref[32 * x + t], local)
    local = jnp.concatenate([local] * (LANES // DIM), axis=1).astype(F32)

    feature = lax.broadcasted_iota(jnp.int32, (DIM, ROWS), 0)
    half = lax.broadcasted_iota(jnp.int32, (DIM, ROWS), 1) // SPAN
    ones = (feature >= LOG_ROW) & (feature < LOG_ROW + 3)

    def key_step(slot, carry):
        seg = segg[slot, pl.ds(0, 1), :].astype(jnp.int32)
        hot = (feature == seg) | (feature == 2 * slot + half + 4) | ones
        rows = pl.ds(pl.multiple_of(slot * ROWS, ROWS), ROWS)
        k_aug[rows, pl.ds(0, DIM)] = kg[slot]
        k_aug[rows, pl.ds(DIM, DIM)] = hot.astype(F32).T.astype(BF16)
        return carry

    key_step(rest, 0)

    def arriving_step(i, carry):
        slot = lax.rem(rest + i, 16)
        arrived(kg.at[slot], r_recv.at[0, slot])
        arrived(segg.at[slot], r_recv.at[1, slot])
        return key_step(slot, carry)

    lax.fori_loop(1, 16, arriving_step, 0)

    document = lax.broadcasted_iota(jnp.int32, (DIM, LANES), 0)

    def query_features(s):
        slot = s // 2
        seg = auxg[slot, pl.ds(s % 2, 1), :].astype(jnp.int32)
        span = auxg[slot, pl.ds(2 + s % 2, 1), :]
        unseen = ((document < 4) & (document != seg)) | (local > span)
        q_aug[s, pl.ds(0, DIM), :] = qg[s].T
        q_aug[s, pl.ds(DIM, DIM), :] = jnp.where(unseen, -1e30, 0.0).astype(BF16)

    def own_step(h, carry):
        s = 2 * x + h
        query_features(s)
        for c in range(0, KEYS, CHUNK):
            scores[pl.ds(c, CHUNK), :] = jnp.dot(
                k_aug[pl.ds(c, CHUNK), :], q_aug[s], preferred_element_type=F32
            )
        rows = pl.ds(pl.multiple_of(rest * ROWS + h * SPAN, SPAN), SPAN)
        later = lax.broadcasted_iota(jnp.int32, (SPAN, LANES), 0) > (
            lax.broadcasted_iota(jnp.int32, (SPAN, LANES), 1) % SPAN
        )
        scores[rows, :] = jnp.where(later, -1e30, scores[rows, :])
        top = jnp.max(scores[...], axis=0, keepdims=True)
        weights = jnp.exp2((scores[...] - top) * (SCALE * LOG2E))
        part[0, pl.ds(s, 1), :] = top
        part[1, pl.ds(s, 1), :] = jnp.sum(weights, axis=0, keepdims=True)
        return carry

    lax.fori_loop(0, 2, own_step, 0)

    def span_step(s, carry):
        query_features(s)
        top = jnp.full((8, LANES), -1e30, F32)
        total = jnp.zeros((8, LANES), F32)
        for c in range(0, KEYS, BLOCK):
            block = jnp.dot(
                k_aug[pl.ds(c, BLOCK), :], q_aug[s], preferred_element_type=F32
            ).reshape(BLOCK // 8, 8, LANES)
            new = jnp.maximum(top, jnp.max(block, axis=0))
            weights = jnp.exp2((block - new) * (SCALE * LOG2E))
            total = total * jnp.exp2((top - new) * (SCALE * LOG2E)) + jnp.sum(weights, axis=0)
            top = new
        whole_top = jnp.max(top, axis=0, keepdims=True)
        total = total * jnp.exp2((top - whole_top) * (SCALE * LOG2E))
        part[0, pl.ds(s, 1), :] = whole_top
        part[1, pl.ds(s, 1), :] = jnp.sum(total, axis=0, keepdims=True)
        return carry

    def rows_step(i, carry):
        slot = lax.rem(x + i, 4)
        pair = pl.ds(pl.multiple_of(2 * slot, 2), 2)
        arrived(qg.at[pair], x_recv.at[0, slot])
        arrived(auxg.at[slot], x_recv.at[2, slot])
        return lax.fori_loop(2 * slot, 2 * slot + 2, span_step, carry)

    lax.fori_loop(1, 4, rows_step, 0)
    early, copies = copies, []
    got[x] = part[...]
    for i, peer in enumerate(xs):
        copies.append(send(part, got.at[x], m_send.at[i], m_recv.at[x], peer))

    def turn_keys(b, carry):
        rows = pl.ds(pl.multiple_of(b * BLOCK, BLOCK), BLOCK)
        kt[b] = k_aug[rows, pl.ds(0, DIM)].T
        return carry

    lax.fori_loop(0, KEYS // BLOCK, turn_keys, 0)
    first_three = (lax.broadcasted_iota(jnp.int32, (ROWS, DIM), 1) < 3).astype(F32).astype(BF16)

    def value_step(slot):
        rows = pl.ds(pl.multiple_of(slot * ROWS, ROWS), ROWS)
        v_aug[rows, pl.ds(0, DIM)] = vg[slot]
        v_aug[rows, pl.ds(DIM, DIM)] = first_three

    def grad_step(s):
        g_aug[s, pl.ds(0, DIM), :] = gg[s].T
        g_aug[s, pl.ds(DIM, 16), :] = pieces_of(-delta[s // 2, pl.ds(s % 2, 1), :])
        g_aug[s, pl.ds(DIM + 16, DIM - 16), :] = jnp.zeros((DIM - 16, LANES), BF16)
        dqt[s] = jnp.zeros((DIM, LANES), F32)

    value_step(rest)
    grad_step(2 * x)
    grad_step(2 * x + 1)

    def arriving_values(i, carry):
        slot = lax.rem(rest + i, 16)
        arrived(vg.at[slot], r_recv.at[2, slot])
        value_step(slot)
        return carry

    lax.fori_loop(1, 16, arriving_values, 0)

    def arriving_grads(i, carry):
        slot = lax.rem(x + i, 4)
        arrived(gg.at[pl.ds(pl.multiple_of(2 * slot, 2), 2)], x_recv.at[1, slot])
        arrived(delta.at[slot], x_recv.at[3, slot])
        grad_step(2 * slot)
        grad_step(2 * slot + 1)
        return carry

    lax.fori_loop(1, 4, arriving_grads, 0)
    for i in range(1, 4):
        slot = lax.rem(x + i, 4)
        arrived(got.at[slot], m_recv.at[slot])
    top = jnp.maximum(
        jnp.maximum(got[0, 0], got[1, 0]), jnp.maximum(got[2, 0], got[3, 0])
    )
    total = jnp.zeros_like(top)
    for slot in range(4):
        total = total + got[slot, 1] * jnp.exp2((got[slot, 0] - top) * (SCALE * LOG2E))
    log_total = top + jnp.log(total) * (1.0 / SCALE)
    for s in range(8):
        q_aug[s, pl.ds(DIM + LOG_ROW, 16), :] = pieces_of(-log_total[s:s + 1])

    for i, peer in enumerate(members):
        copies.append(
            send(act_piece(act_ref, member + SHIFTS[i]), act_in.at[i + 1], act_send.at[i],
                 act_recv.at[i], peer)
        )

    def tile(pair, s, masked):
        rows = pl.ds(pl.multiple_of(pair * BLOCK, BLOCK), BLOCK)
        probs = jnp.exp2(
            jnp.dot(k_aug[rows, :], q_aug[s], preferred_element_type=F32) * (SCALE * LOG2E)
        )
        if masked:
            key = lax.broadcasted_iota(jnp.int32, (BLOCK, LANES), 0) - (
                rest % 2 * ROWS + s % 2 * SPAN
            )
            key = jnp.where(s // 2 == x, key, SPAN)
            row = lax.broadcasted_iota(jnp.int32, (BLOCK, LANES), 1) % SPAN
            probs = jnp.where((key < SPAN) & (key > row), 0.0, probs)
        prob_grad = jnp.dot(v_aug[rows, :], g_aug[s], preferred_element_type=F32)
        score_grad = (probs * prob_grad * SCALE).astype(BF16)
        dv_acc[...] += jnp.dot(probs.astype(BF16), gg[s], preferred_element_type=F32)
        dk_acc[...] += jnp.dot(score_grad, qg[s], preferred_element_type=F32)
        dqt[s] += jnp.dot(kt[pair], score_grad, preferred_element_type=F32)

    def key_block(pair):
        dk_acc[...] = jnp.zeros_like(dk_acc)
        dv_acc[...] = jnp.zeros_like(dv_acc)

        def query_step(t, carry):
            diagonal = (t == x // 2) & (pair == rest // 2)

            @pl.when(diagonal)
            def _():
                for u in range(4):
                    tile(pair, 4 * t + u, True)

            @pl.when(jnp.logical_not(diagonal))
            def _():
                for u in range(4):
                    tile(pair, 4 * t + u, False)

            return carry

        lax.fori_loop(0, 2, query_step, 0)
        for h in range(2):
            dkv_out[2 * pair + h, 0] = dk_acc[pl.ds(h * ROWS, ROWS), :].astype(BF16)
            dkv_out[2 * pair + h, 1] = dv_acc[pl.ds(h * ROWS, ROWS), :].astype(BF16)

    def block_of(b):
        turn = b // 2
        offset = (2 + turn + 5 * (turn // 2) + 2 * (turn // 3)) % 4 + 4 * ((b + b // 6) % 2)
        return lax.rem(rest // 2 + offset, 8)

    def to_holder(b, h):
        slot = 2 * block_of(b) + h
        return pltpu.make_async_remote_copy(
            src_ref=dkv_out.at[slot], dst_ref=dkv_in.at[rest], send_sem=d_send.at[2 * b + h],
            recv_sem=d_recv.at[rest], device_id=(x * 16 + slot, dp), device_id_type=MESH,
        )

    def block_step(b, carry):
        key_block(block_of(b))
        to_holder(b, 0).start()
        to_holder(b, 1).start()
        return carry

    lax.fori_loop(0, 7, block_step, 0)
    key_block(rest // 2)
    other = rest + 1 - 2 * (rest % 2)
    copies.append(
        send(dkv_out.at[other], dkv_in.at[rest], d_send.at[14], d_recv.at[rest],
             (x * 16 + other, dp))
    )
    dkv_in[rest] = dkv_out[rest]

    for copy in early:
        copy.wait_send()

    def turn_queries(s, carry):
        dq_out[s] = dqt[s].T.astype(BF16)
        return carry

    lax.fori_loop(0, 8, turn_queries, 0)
    dq_in[x] = dq_out[two]

    for i in range(1, 16):
        slot = lax.rem(rest + i, 16)
        arrived(dkv_in.at[slot], d_recv.at[slot])
    for p in range(2):
        summed = dkv_in[0, p].astype(F32)
        for slot in range(1, 16):
            summed = summed + dkv_in[slot, p].astype(F32)
        kv_low = summed.astype(BF16)
        kv_in[p, 0] = kv_low
        kvgrad_ref[:, pl.ds(p * DIM, DIM)] = kv_low
        for i, peer in enumerate(members):
            copies.append(
                send(kv_in.at[p, 0], kv_in.at[p, i + 1], kv_send.at[p, i], kv_recv.at[p, i], peer)
            )
    for i, peer in enumerate(xs):
        there = lax.rem(x + i + 1, 4)
        copies.append(
            send(dq_out.at[pl.ds(pl.multiple_of(2 * there, 2), 2)], dq_in.at[x], dq_send.at[i],
                 dq_recv.at[x], peer)
        )

    here = y_lo == core

    def to_owner(p, i):
        there_z = lax.rem(z + i // 4, 8)
        there_dp = lax.rem(dp + i % 4, 4)
        rows = pl.ds(pl.multiple_of((there_z * 4 + there_dp) * 32, 32), 32)
        return pltpu.make_async_remote_copy(
            src_ref=partial.at[p, rows], dst_ref=g_in.at[p, line], send_sem=gr_send.at[p, i],
            recv_sem=gr_recv.at[p, line],
            device_id=(x * 16 + core * 8 + there_z, there_dp), device_id_type=MESH,
        )

    own_rows = pl.ds(pl.multiple_of((z * 4 + dp) * 32, 32), 32)
    for i in range(GROUP - 1):
        arrived(act_in.at[i + 1], act_recv.at[i])
    for p in range(2):
        total = jnp.zeros((DIM, FEATURES), F32)
        for i in range(GROUP):
            if i > 0:
                arrived(kv_in.at[p, i], kv_recv.at[p, i - 1])
            total = total + jnp.dot(kv_in[p, i].T, act_in[i], preferred_element_type=F32)
        partial[p] = total.T.astype(BF16)
        for i in range(1, OWNERS):
            to_owner(p, i).start()

        @pl.when(here)
        def _():
            pltpu.make_async_copy(
                partial.at[p, own_rows], g_in.at[p, line], gr_recv.at[p, line]
            ).start()

        @pl.when(jnp.logical_not(here))
        def _():
            to_owner(p, 0).start()

    for copy in copies:
        copy.wait_send()
    copies = []
    for b in range(7):
        to_holder(b, 0).wait_send()
        to_holder(b, 1).wait_send()

    for i in range(1, 4):
        slot = lax.rem(x + i, 4)
        arrived(dq_in.at[slot], dq_recv.at[slot])
    for span in range(2):
        for h in range(HEADS):
            rows = pl.ds(h * SPAN, SPAN)
            summed = dq_in[0, span, rows, :].astype(F32)
            for slot in range(1, 4):
                summed = summed + dq_in[slot, span, rows, :].astype(F32)
            qgrad_ref[pl.ds(span * SPAN, SPAN), pl.ds(h * DIM, DIM)] = summed.astype(BF16)

    sums = []
    for p in range(2):
        for slot in range(OWNERS):
            arrived(g_in.at[p, slot], gr_recv.at[p, slot])
        grad = g_in[p, 0].astype(F32)
        for slot in range(1, OWNERS):
            grad = grad + g_in[p, slot].astype(F32)
        weight = w_ref[p]
        one = beta_one * m1_ref[p] + (1.0 - beta_one) * grad
        two = beta_two * m2_ref[p] + (1.0 - beta_two) * grad * grad
        n1_ref[p] = one
        n2_ref[p] = two
        update = one / (jnp.sqrt(two) + epsilon) + weight_decay * weight
        update_ref[p] = update
        sums.append(jnp.sum(weight * weight, axis=0, keepdims=True))
        sums.append(jnp.sum(update * update, axis=0, keepdims=True))
    a_msg[...] = jnp.concatenate(sums + [jnp.zeros((4, DIM), F32)], axis=0)
    a_in[member] = a_msg[...]
    for i, peer in enumerate(members):
        copies.append(send(a_msg, a_in.at[member], a_send.at[i], a_recv.at[member], peer))

    for i in range(1, GROUP):
        slot = lax.rem(member + i, GROUP)
        arrived(a_in.at[slot], a_recv.at[slot])
    summed = a_in[0]
    for slot in range(1, GROUP):
        summed = summed + a_in[slot]
    b_msg[...] = summed
    b_in[line] = summed
    late = [
        send(b_msg, b_in.at[line], b_send.at[i], b_recv.at[line], peer)
        for i, peer in enumerate(lines)
    ]
    for copy in copies:
        copy.wait_send()
    for p in range(2):
        for i in range(1, OWNERS):
            to_owner(p, i).wait_send()

        @pl.when(jnp.logical_not(here))
        def _():
            to_owner(p, 0).wait_send()

    for i in range(1, OWNERS):
        slot = lax.rem(line + i, OWNERS)
        arrived(b_in.at[slot], b_recv.at[slot])
    summed = b_in[0]
    for slot in range(1, OWNERS):
        summed = summed + b_in[slot]
    norms = jnp.sqrt(jnp.sum(summed, axis=1, keepdims=True))
    ratios = []
    for p in range(2):
        ratio = norms[2 * p:2 * p + 1] / (norms[2 * p + 1:2 * p + 2] + epsilon)
        ratios.append(ratio)
    trust_ref[...] = jnp.concatenate(
        [jnp.broadcast_to(ratio, (1, DIM)) for ratio in ratios] + [jnp.zeros((6, DIM), F32)], axis=0
    )
    for copy in late:
        copy.wait_send()


def whole(span_order, queries, out_grad, attn_out, key_states, value_states, act, segment_ids,
          kv_weight, moment_one, moment_two):
    state = jax.ShapeDtypeStruct((2, 32, DIM), F32)
    dma = pltpu.SemaphoreType.DMA
    return pl.pallas_call(
        whole_kernel,
        out_shape=(
            jax.ShapeDtypeStruct((ROWS, HEADS * DIM), BF16),
            jax.ShapeDtypeStruct((ROWS, 2 * DIM), BF16),
            state, state, state,
            jax.ShapeDtypeStruct((8, DIM), F32),
        ),
        in_specs=[smem_spec()] + [any_spec()] * 6 + [vmem_spec()] + [any_spec()] * 3,
        out_specs=(vmem_spec(),) * 6,
        scratch_shapes=[
            VMEM((2, 32, DIM), F32),
            VMEM((2, 32, DIM), F32),
            VMEM((2, 32, DIM), F32),
            VMEM((ROWS, HEADS * DIM), BF16),
            VMEM((ROWS, HEADS * DIM), BF16),
            VMEM((ROWS, HEADS * DIM), BF16),
            VMEM((8, LANES, DIM), BF16),
            VMEM((8, LANES, DIM), BF16),
            VMEM((16, ROWS, DIM), BF16),
            VMEM((16, ROWS, DIM), BF16),
            VMEM((4, 8, LANES), F32),
            VMEM((4, 8, LANES), F32),
            VMEM((16, 8, ROWS), F32),
            VMEM((KEYS, 2 * DIM), BF16),
            VMEM((KEYS, 2 * DIM), BF16),
            VMEM((8, 2 * DIM, LANES), BF16),
            VMEM((8, 2 * DIM, LANES), BF16),
            VMEM((KEYS // BLOCK, DIM, BLOCK), BF16),
            VMEM((KEYS, LANES), F32),
            VMEM((2, 8, LANES), F32),
            VMEM((4, 2, 8, LANES), F32),
            VMEM((BLOCK, DIM), F32),
            VMEM((BLOCK, DIM), F32),
            VMEM((8, DIM, LANES), F32),
            VMEM((16, 2, ROWS, DIM), BF16),
            VMEM((16, 2, ROWS, DIM), BF16),
            VMEM((8, LANES, DIM), BF16),
            VMEM((4, 2, LANES, DIM), BF16),
            VMEM((GROUP, ROWS, FEATURES), BF16),
            VMEM((2, GROUP, ROWS, DIM), BF16),
            VMEM((2, FEATURES, DIM), BF16),
            VMEM((2, OWNERS, 32, DIM), BF16),
            VMEM((GROUP, 8, DIM), F32),
            VMEM((8, DIM), F32),
            VMEM((OWNERS, 8, DIM), F32),
            VMEM((8, DIM), F32),
            dma((4, 3)), dma((4, 4)),
            dma((3, 15)), dma((3, 16)),
            dma((7,)), dma((7,)),
            dma((3,)), dma((4,)),
            dma((15,)), dma((16,)),
            dma((3,)), dma((4,)),
            dma((2, 7)), dma((2, 7)),
            dma((2, OWNERS)), dma((2, OWNERS)),
            dma((7,)), dma((GROUP,)),
            dma((31,)), dma((OWNERS,)),
            dma((9,)),
        ],
        compiler_params=pltpu.CompilerParams(
            collective_id=0, has_side_effects=True, vmem_limit_bytes=VMEM_LIMIT
        ),
        name="attention_backward",
    )(span_order, queries, out_grad, attn_out, key_states, value_states, act, segment_ids,
      kv_weight, moment_one, moment_two)


def finish_kernel(
    q_ref, kv_ref, update_ref, one_ref, two_ref, ratio_ref, weight_ref,
    qgrad_ref, kvgrad_ref, nw_ref, n1_ref, n2_ref, trust_ref,
):
    qgrad_ref[0] = q_ref[...]
    kvgrad_ref[0] = kv_ref[...]
    n1_ref[...] = one_ref[...]
    n2_ref[...] = two_ref[...]
    for p in range(2):
        ratio = ratio_ref[pl.ds(p, 1), :]
        trust_ref[p] = ratio[0, 0]
        nw_ref[p] = weight_ref[p] - learn_rate * ratio * update_ref[p]


def finish(query_grad, kv_grad, update, new_one, new_two, ratio, kv_weight):
    state = jax.ShapeDtypeStruct((2, 32, DIM), F32)
    return pl.pallas_call(
        finish_kernel,
        out_shape=(
            jax.ShapeDtypeStruct((1, ROWS, HEADS * DIM), BF16),
            jax.ShapeDtypeStruct((1, ROWS, 2 * DIM), BF16),
            state, state, state,
            jax.ShapeDtypeStruct((2,), F32),
        ),
        in_specs=[vmem_spec()] * 7,
        out_specs=(vmem_spec(),) * 5 + (smem_spec(),),
        compiler_params=pltpu.CompilerParams(vmem_limit_bytes=VMEM_LIMIT),
        name="new_weights",
    )(query_grad, kv_grad, update, new_one, new_two, ratio, kv_weight)


def on_device(
    queries,
    key_states,
    value_states,
    attn_out,
    out_grad,
    activations,
    segment_ids,
    span_order,
    kv_weight,
    moment_one,
    moment_two,
):
    query_grad, kv_grad, update, new_one, new_two, trust = whole(
        span_order, queries[0], out_grad[0], attn_out[0], key_states[0], value_states[0],
        activations[0], segment_ids, kv_weight, moment_one, moment_two,
    )
    return finish(query_grad, kv_grad, update, new_one, new_two, trust, kv_weight)


def solution(mesh):
    in_specs = (
        P("dp", "context", None),
        P("dp", "context", None),
        P("dp", "context", None),
        P("dp", "context", None),
        P("dp", "context", None),
        P("dp", "context", None),
        P("dp", "context"),
        P(),
        P(None, ("context", "dp"), None),
        P(None, ("context", "dp"), None),
        P(None, ("context", "dp"), None),
    )
    out_specs = (
        P("dp", "context", None),
        P("dp", "context", None),
        P(None, ("context", "dp"), None),
        P(None, ("context", "dp"), None),
        P(None, ("context", "dp"), None),
        P(),
    )
    return jax.shard_map(
        on_device, mesh=mesh, in_specs=in_specs, out_specs=out_specs, check_vma=False
    )
```

```python
import functools

import jax
import jax.numpy as jnp
from jax import lax
from jax.experimental import pallas as pl
from jax.experimental.pallas import tpu as pltpu
from jax.sharding import PartitionSpec as P

beta_one = 0.9
beta_two = 0.999
epsilon = 1e-06
weight_decay = 0.01
learn_rate = 0.01

HEADS = 8
DIM = 128
SPAN = 64
ROWS = 128
LANES = HEADS * SPAN
BLOCK = 256
KEYS = 2048
LOG_ROW = 48
GROUP = 8
FEATURES = 1024
OWNERS = 32
FAR_FIRST = sorted(
    range(1, OWNERS), key=lambda i: -min(i // 2 % 8, 8 - i // 2 % 8) - (0, 2, 1, 1)[i // 16 * 2 + i % 2]
)
SHIFTS = (1, 7, 2, 6, 3, 5, 4)
CHUNK = 512
VMEM_LIMIT = 62 * 1024 * 1024
SCALE = DIM ** (-0.5)
LOG2E = 1.4426950408889634
MESH = pl.DeviceIdType.MESH
VMEM = pltpu.VMEM
F32 = jnp.float32
BF16 = jnp.bfloat16


def vmem_spec():
    return pl.BlockSpec(memory_space=pltpu.VMEM)


def any_spec():
    return pl.BlockSpec(memory_space=pl.ANY)


def smem_spec():
    return pl.BlockSpec(memory_space=pltpu.SMEM)


def greet(peers):
    barrier = pltpu.get_barrier_semaphore()
    for peer in peers:
        pl.semaphore_signal(barrier, inc=1, device_id=peer, device_id_type=MESH)
    return barrier


def send(src, dst, send_sem, recv_sem, peer):
    copy = pltpu.make_async_remote_copy(
        src_ref=src, dst_ref=dst, send_sem=send_sem, recv_sem=recv_sem,
        device_id=peer, device_id_type=MESH,
    )
    copy.start()
    return copy


def arrived(dst, sem):
    pltpu.make_async_copy(dst, dst, sem).wait()


def place():
    me = lax.axis_index("context")
    dp = lax.axis_index("dp")
    return me, dp, me // 16, me % 16


def x_peers(me, dp, x, rest):
    return [(lax.rem(x + i, 4) * 16 + rest, dp) for i in range(1, 4)]


def rest_peers(me, dp, x, rest):
    return [(x * 16 + lax.rem(rest + i, 16), dp) for i in range(1, 16)]


def member_peers(me, dp):
    member = me // 16 * 2 + dp % 2
    peers = []
    for shift in SHIFTS:
        there = lax.rem(member + shift, GROUP)
        peers.append((there // 2 * 16 + me % 16, dp // 2 * 2 + there % 2))
    return member, peers


def act_piece(act_ref, index):
    there = lax.rem(index, GROUP)
    return act_ref.at[:, pl.ds(pl.multiple_of(there * FEATURES, FEATURES), FEATURES)]


def pieces_of(value):
    first = value.astype(BF16)
    left = value - first.astype(F32)
    second = left.astype(BF16)
    third = (left - second.astype(F32)).astype(BF16)
    zeros = jnp.zeros((13, value.shape[1]), F32)
    return jnp.concatenate(
        [first.astype(F32), second.astype(F32), third.astype(F32), zeros], axis=0
    ).astype(BF16)


def whole_kernel(
    order_ref, q_ref, g_ref, o_ref, k_ref, v_ref, act_ref, seg_ref, w_hbm, m1_hbm, m2_hbm,
    qgrad_ref, kvgrad_ref, update_ref, n1_ref, n2_ref, trust_ref,
    w_ref, m1_ref, m2_ref, q_own, g_own, o_own, qg, gg, kg, vg, auxg, delta, segg, k_aug, v_aug, q_aug, g_aug, kt,
    scores, part, got, dk_acc, dv_acc, dqt, dkv_out, dkv_in, dq_out, dq_in,
    act_in, kv_in, partial, g_in, a_in, a_msg, b_in, b_msg,
    x_send, x_recv, r_send, r_recv, act_send, act_recv, m_send, m_recv,
    d_send, d_recv, dq_send, dq_recv, kv_send, kv_recv,
    gr_send, gr_recv, a_send, a_recv, b_send, b_recv, own_sem,
):
    me, dp, x, rest = place()
    y_lo, z = rest // 8, rest % 8
    y_hi, core = dp // 2, dp % 2
    line = rest * 2 + y_hi
    xs = x_peers(me, dp, x, rest)
    rs = rest_peers(me, dp, x, rest)
    member, members = member_peers(me, dp)
    two = pl.ds(pl.multiple_of(2 * x, 2), 2)

    def in_line(index):
        return (x * 16 + index // 2, index % 2 * 2 + core)

    lines = [in_line(lax.rem(line + i, OWNERS)) for i in FAR_FIRST]
    own = [
        pltpu.make_async_copy(q_ref, q_own, own_sem.at[2]),
        pltpu.make_async_copy(k_ref, kg.at[rest], own_sem.at[0]),
        pltpu.make_async_copy(g_ref, g_own, own_sem.at[3]),
        pltpu.make_async_copy(o_ref, o_own, own_sem.at[4]),
        pltpu.make_async_copy(v_ref, vg.at[rest], own_sem.at[5]),
        pltpu.make_async_copy(act_piece(act_ref, member), act_in.at[0], own_sem.at[1]),
        pltpu.make_async_copy(w_hbm, w_ref, own_sem.at[6]),
        pltpu.make_async_copy(m1_hbm, m1_ref, own_sem.at[7]),
        pltpu.make_async_copy(m2_hbm, m2_ref, own_sem.at[8]),
    ]
    for copy in own:
        copy.start()
    greeted = [
        (x * 16 + lax.rem(rest + i // 4, 16), lax.rem(dp + i % 4, 4)) for i in range(1, 64)
    ]
    greeted += [
        (lax.rem(x + i, 4) * 16 + rest, y_hi * 2 + j) for i in range(1, 4) for j in range(2)
    ]
    barrier = greet(greeted)
    seg_own = jnp.broadcast_to(seg_ref[...], (8, ROWS)).astype(F32)
    segg[rest] = seg_own
    swapped = pltpu.roll(seg_own, SPAN, 1)
    lower = lax.broadcasted_iota(jnp.int32, (8, ROWS), 1) < SPAN
    row_of = lax.broadcasted_iota(jnp.int32, (8, LANES), 0)
    auxg[x] = jnp.where(
        row_of == 0, jnp.concatenate([jnp.where(lower, seg_own, swapped)] * 4, axis=1),
        jnp.where(
            row_of == 1, jnp.concatenate([jnp.where(lower, swapped, seg_own)] * 4, axis=1),
            jnp.where(row_of == 2, order_ref[2 * me], order_ref[2 * me + 1]).astype(F32),
        ),
    )
    own[0].wait()
    own[1].wait()
    for span in range(2):
        for h in range(HEADS):
            qg[2 * x + span, pl.ds(h * SPAN, SPAN), :] = q_own[
                pl.ds(span * SPAN, SPAN), pl.ds(h * DIM, DIM)
            ]
    pl.semaphore_wait(barrier, len(greeted))

    copies = []
    for i, peer in enumerate(rs):
        if i < 3:
            copies.append(send(qg.at[two], qg.at[two], x_send.at[0, i], x_recv.at[0, x], xs[i]))
            copies.append(send(auxg.at[x], auxg.at[x], x_send.at[2, i], x_recv.at[2, x], xs[i]))
        copies.append(send(kg.at[rest], kg.at[rest], r_send.at[0, i], r_recv.at[0, rest], peer))
        copies.append(send(segg.at[rest], segg.at[rest], r_send.at[1, i], r_recv.at[1, rest], peer))
    for copy in own[2:]:
        copy.wait()
    for span in range(2):
        for h in range(HEADS):
            gg[2 * x + span, pl.ds(h * SPAN, SPAN), :] = g_own[
                pl.ds(span * SPAN, SPAN), pl.ds(h * DIM, DIM)
            ]
    for i, peer in enumerate(rs):
        if i < 3:
            copies.append(send(gg.at[two], gg.at[two], x_send.at[1, i], x_recv.at[1, x], xs[i]))
        copies.append(send(vg.at[rest], vg.at[rest], r_send.at[2, i], r_recv.at[2, rest], peer))
    delta[x] = jnp.zeros((8, LANES), F32)
    for span in range(2):
        rows = pl.ds(span * SPAN, SPAN)
        products = []
        for h in range(HEADS):
            cols = pl.ds(h * DIM, DIM)
            products.append(g_own[rows, cols].astype(F32) * o_own[rows, cols].astype(F32))
        product = jnp.concatenate(products, axis=0)
        delta[x, pl.ds(span, 1), :] = jnp.sum(product.T, axis=0, keepdims=True)
    for i, peer in enumerate(xs):
        copies.append(send(delta.at[x], delta.at[x], x_send.at[3, i], x_recv.at[3, x], peer))
    span_row = lax.broadcasted_iota(jnp.int32, (DIM, DIM), 0)
    local = jnp.full((DIM, DIM), -1, jnp.int32)
    for t in range(32):
        local = jnp.where(span_row == t + 4, order_ref[32 * x + t], local)
    local = jnp.concatenate([local] * (LANES // DIM), axis=1).astype(F32)

    feature = lax.broadcasted_iota(jnp.int32, (DIM, ROWS), 0)
    half = lax.broadcasted_iota(jnp.int32, (DIM, ROWS), 1) // SPAN
    ones = (feature >= LOG_ROW) & (feature < LOG_ROW + 3)

    def key_step(slot, carry):
        seg = segg[slot, pl.ds(0, 1), :].astype(jnp.int32)
        hot = (feature == seg) | (feature == 2 * slot + half + 4) | ones
        rows = pl.ds(pl.multiple_of(slot * ROWS, ROWS), ROWS)
        k_aug[rows, pl.ds(0, DIM)] = kg[slot]
        k_aug[rows, pl.ds(DIM, DIM)] = hot.astype(F32).T.astype(BF16)
        return carry

    key_step(rest, 0)

    def arriving_step(i, carry):
        slot = lax.rem(rest + i, 16)
        arrived(kg.at[slot], r_recv.at[0, slot])
        arrived(segg.at[slot], r_recv.at[1, slot])
        return key_step(slot, carry)

    lax.fori_loop(1, 16, arriving_step, 0)

    document = lax.broadcasted_iota(jnp.int32, (DIM, LANES), 0)

    def query_features(s):
        slot = s // 2
        seg = auxg[slot, pl.ds(s % 2, 1), :].astype(jnp.int32)
        span = auxg[slot, pl.ds(2 + s % 2, 1), :]
        unseen = ((document < 4) & (document != seg)) | (local > span)
        q_aug[s, pl.ds(0, DIM), :] = qg[s].T
        q_aug[s, pl.ds(DIM, DIM), :] = jnp.where(unseen, -1e30, 0.0).astype(BF16)

    def own_step(h, carry):
        s = 2 * x + h
        query_features(s)
        for c in range(0, KEYS, CHUNK):
            scores[pl.ds(c, CHUNK), :] = jnp.dot(
                k_aug[pl.ds(c, CHUNK), :], q_aug[s], preferred_element_type=F32
            )
        rows = pl.ds(pl.multiple_of(rest * ROWS + h * SPAN, SPAN), SPAN)
        later = lax.broadcasted_iota(jnp.int32, (SPAN, LANES), 0) > (
            lax.broadcasted_iota(jnp.int32, (SPAN, LANES), 1) % SPAN
        )
        scores[rows, :] = jnp.where(later, -1e30, scores[rows, :])
        top = jnp.max(scores[...], axis=0, keepdims=True)
        weights = jnp.exp2((scores[...] - top) * (SCALE * LOG2E))
        part[0, pl.ds(s, 1), :] = top
        part[1, pl.ds(s, 1), :] = jnp.sum(weights, axis=0, keepdims=True)
        return carry

    lax.fori_loop(0, 2, own_step, 0)

    def span_step(s, carry):
        query_features(s)
        top = jnp.full((8, LANES), -1e30, F32)
        total = jnp.zeros((8, LANES), F32)
        for c in range(0, KEYS, BLOCK):
            block = jnp.dot(
                k_aug[pl.ds(c, BLOCK), :], q_aug[s], preferred_element_type=F32
            ).reshape(BLOCK // 8, 8, LANES)
            new = jnp.maximum(top, jnp.max(block, axis=0))
            weights = jnp.exp2((block - new) * (SCALE * LOG2E))
            total = total * jnp.exp2((top - new) * (SCALE * LOG2E)) + jnp.sum(weights, axis=0)
            top = new
        whole_top = jnp.max(top, axis=0, keepdims=True)
        total = total * jnp.exp2((top - whole_top) * (SCALE * LOG2E))
        part[0, pl.ds(s, 1), :] = whole_top
        part[1, pl.ds(s, 1), :] = jnp.sum(total, axis=0, keepdims=True)
        return carry

    def rows_step(i, carry):
        slot = lax.rem(x + i, 4)
        pair = pl.ds(pl.multiple_of(2 * slot, 2), 2)
        arrived(qg.at[pair], x_recv.at[0, slot])
        arrived(auxg.at[slot], x_recv.at[2, slot])
        return lax.fori_loop(2 * slot, 2 * slot + 2, span_step, carry)

    lax.fori_loop(1, 4, rows_step, 0)
    early, copies = copies, []
    got[x] = part[...]
    for i, peer in enumerate(xs):
        copies.append(send(part, got.at[x], m_send.at[i], m_recv.at[x], peer))

    def turn_keys(b, carry):
        rows = pl.ds(pl.multiple_of(b * BLOCK, BLOCK), BLOCK)
        kt[b] = k_aug[rows, pl.ds(0, DIM)].T
        return carry

    lax.fori_loop(0, KEYS // BLOCK, turn_keys, 0)
    first_three = (lax.broadcasted_iota(jnp.int32, (ROWS, DIM), 1) < 3).astype(F32).astype(BF16)

    def value_step(slot):
        rows = pl.ds(pl.multiple_of(slot * ROWS, ROWS), ROWS)
        v_aug[rows, pl.ds(0, DIM)] = vg[slot]
        v_aug[rows, pl.ds(DIM, DIM)] = first_three

    def grad_step(s):
        g_aug[s, pl.ds(0, DIM), :] = gg[s].T
        g_aug[s, pl.ds(DIM, 16), :] = pieces_of(-delta[s // 2, pl.ds(s % 2, 1), :])
        g_aug[s, pl.ds(DIM + 16, DIM - 16), :] = jnp.zeros((DIM - 16, LANES), BF16)
        dqt[s] = jnp.zeros((DIM, LANES), F32)

    value_step(rest)
    grad_step(2 * x)
    grad_step(2 * x + 1)

    def arriving_values(i, carry):
        slot = lax.rem(rest + i, 16)
        arrived(vg.at[slot], r_recv.at[2, slot])
        value_step(slot)
        return carry

    lax.fori_loop(1, 16, arriving_values, 0)

    def arriving_grads(i, carry):
        slot = lax.rem(x + i, 4)
        arrived(gg.at[pl.ds(pl.multiple_of(2 * slot, 2), 2)], x_recv.at[1, slot])
        arrived(delta.at[slot], x_recv.at[3, slot])
        grad_step(2 * slot)
        grad_step(2 * slot + 1)
        return carry

    lax.fori_loop(1, 4, arriving_grads, 0)
    for i in range(1, 4):
        slot = lax.rem(x + i, 4)
        arrived(got.at[slot], m_recv.at[slot])
    top = jnp.maximum(
        jnp.maximum(got[0, 0], got[1, 0]), jnp.maximum(got[2, 0], got[3, 0])
    )
    total = jnp.zeros_like(top)
    for slot in range(4):
        total = total + got[slot, 1] * jnp.exp2((got[slot, 0] - top) * (SCALE * LOG2E))
    log_total = top + jnp.log(total) * (1.0 / SCALE)
    for s in range(8):
        q_aug[s, pl.ds(DIM + LOG_ROW, 16), :] = pieces_of(-log_total[s:s + 1])

    for i, peer in enumerate(members):
        copies.append(
            send(act_piece(act_ref, member + SHIFTS[i]), act_in.at[i + 1], act_send.at[i],
                 act_recv.at[i], peer)
        )

    def tile(pair, s, masked):
        rows = pl.ds(pl.multiple_of(pair * BLOCK, BLOCK), BLOCK)
        probs = jnp.exp2(
            jnp.dot(k_aug[rows, :], q_aug[s], preferred_element_type=F32) * (SCALE * LOG2E)
        )
        if masked:
            key = lax.broadcasted_iota(jnp.int32, (BLOCK, LANES), 0) - (
                rest % 2 * ROWS + s % 2 * SPAN
            )
            key = jnp.where(s // 2 == x, key, SPAN)
            row = lax.broadcasted_iota(jnp.int32, (BLOCK, LANES), 1) % SPAN
            probs = jnp.where((key < SPAN) & (key > row), 0.0, probs)
        prob_grad = jnp.dot(v_aug[rows, :], g_aug[s], preferred_element_type=F32)
        score_grad = (probs * prob_grad * SCALE).astype(BF16)
        dv_acc[...] += jnp.dot(probs.astype(BF16), gg[s], preferred_element_type=F32)
        dk_acc[...] += jnp.dot(score_grad, qg[s], preferred_element_type=F32)
        dqt[s] += jnp.dot(kt[pair], score_grad, preferred_element_type=F32)

    def key_block(pair, own):
        dk_acc[...] = jnp.zeros_like(dk_acc)
        dv_acc[...] = jnp.zeros_like(dv_acc)

        def query_step(t, carry):
            diagonal = t == x // 2

            @pl.when(diagonal)
            def _():
                for u in range(4):
                    tile(pair, 4 * t + u, True)

            @pl.when(jnp.logical_not(diagonal))
            def _():
                for u in range(4):
                    tile(pair, 4 * t + u, False)

            return carry

        if own:
            lax.fori_loop(0, 2, query_step, 0)
        else:
            for s in range(8):
                tile(pair, s, False)
        for h in range(2):
            dkv_out[2 * pair + h, 0] = dk_acc[pl.ds(h * ROWS, ROWS), :].astype(BF16)
            dkv_out[2 * pair + h, 1] = dv_acc[pl.ds(h * ROWS, ROWS), :].astype(BF16)

    def block_of(b):
        turn = b // 2
        offset = (2 + turn + 5 * (turn // 2) + 2 * (turn // 3)) % 4 + 4 * ((b + b // 6) % 2)
        return lax.rem(rest // 2 + offset, 8)

    def to_holder(b, h):
        slot = 2 * block_of(b) + h
        return pltpu.make_async_remote_copy(
            src_ref=dkv_out.at[slot], dst_ref=dkv_in.at[rest], send_sem=d_send.at[2 * b + h],
            recv_sem=d_recv.at[rest], device_id=(x * 16 + slot, dp), device_id_type=MESH,
        )

    def block_step(b, carry):
        key_block(block_of(b), False)
        to_holder(b, 0).start()
        to_holder(b, 1).start()
        return carry

    lax.fori_loop(0, 7, block_step, 0)
    key_block(rest // 2, True)
    other = rest + 1 - 2 * (rest % 2)
    copies.append(
        send(dkv_out.at[other], dkv_in.at[rest], d_send.at[14], d_recv.at[rest],
             (x * 16 + other, dp))
    )
    dkv_in[rest] = dkv_out[rest]

    for copy in early:
        copy.wait_send()

    def turn_queries(s, carry):
        dq_out[s] = dqt[s].T.astype(BF16)
        return carry

    lax.fori_loop(0, 8, turn_queries, 0)
    dq_in[x] = dq_out[two]

    for i in range(1, 16):
        slot = lax.rem(rest + i, 16)
        arrived(dkv_in.at[slot], d_recv.at[slot])
    for p in range(2):
        summed = dkv_in[0, p].astype(F32)
        for slot in range(1, 16):
            summed = summed + dkv_in[slot, p].astype(F32)
        kv_low = summed.astype(BF16)
        kv_in[p, 0] = kv_low
        kvgrad_ref[:, pl.ds(p * DIM, DIM)] = kv_low
        for i, peer in enumerate(members):
            copies.append(
                send(kv_in.at[p, 0], kv_in.at[p, i + 1], kv_send.at[p, i], kv_recv.at[p, i], peer)
            )
    for i, peer in enumerate(xs):
        there = lax.rem(x + i + 1, 4)
        copies.append(
            send(dq_out.at[pl.ds(pl.multiple_of(2 * there, 2), 2)], dq_in.at[x], dq_send.at[i],
                 dq_recv.at[x], peer)
        )

    here = y_lo == core

    def to_owner(p, i):
        there_z = lax.rem(z + i // 4, 8)
        there_dp = lax.rem(dp + i % 4, 4)
        rows = pl.ds(pl.multiple_of((there_z * 4 + there_dp) * 32, 32), 32)
        return pltpu.make_async_remote_copy(
            src_ref=partial.at[p, rows], dst_ref=g_in.at[p, line], send_sem=gr_send.at[p, i],
            recv_sem=gr_recv.at[p, line],
            device_id=(x * 16 + core * 8 + there_z, there_dp), device_id_type=MESH,
        )

    own_rows = pl.ds(pl.multiple_of((z * 4 + dp) * 32, 32), 32)
    for i in range(GROUP - 1):
        arrived(act_in.at[i + 1], act_recv.at[i])
    for p in range(2):
        total = jnp.zeros((DIM, FEATURES), F32)
        for i in range(GROUP):
            if i > 0:
                arrived(kv_in.at[p, i], kv_recv.at[p, i - 1])
            total = total + jnp.dot(kv_in[p, i].T, act_in[i], preferred_element_type=F32)
        partial[p] = total.T.astype(BF16)
        for i in range(1, OWNERS):
            to_owner(p, i).start()

        @pl.when(here)
        def _():
            pltpu.make_async_copy(
                partial.at[p, own_rows], g_in.at[p, line], gr_recv.at[p, line]
            ).start()

        @pl.when(jnp.logical_not(here))
        def _():
            to_owner(p, 0).start()

    for copy in copies:
        copy.wait_send()
    copies = []
    for b in range(7):
        to_holder(b, 0).wait_send()
        to_holder(b, 1).wait_send()

    for i in range(1, 4):
        slot = lax.rem(x + i, 4)
        arrived(dq_in.at[slot], dq_recv.at[slot])
    for span in range(2):
        for h in range(HEADS):
            rows = pl.ds(h * SPAN, SPAN)
            summed = dq_in[0, span, rows, :].astype(F32)
            for slot in range(1, 4):
                summed = summed + dq_in[slot, span, rows, :].astype(F32)
            qgrad_ref[pl.ds(span * SPAN, SPAN), pl.ds(h * DIM, DIM)] = summed.astype(BF16)

    sums = []
    for p in range(2):
        for slot in range(OWNERS):
            arrived(g_in.at[p, slot], gr_recv.at[p, slot])
        grad = g_in[p, 0].astype(F32)
        for slot in range(1, OWNERS):
            grad = grad + g_in[p, slot].astype(F32)
        weight = w_ref[p]
        one = beta_one * m1_ref[p] + (1.0 - beta_one) * grad
        two = beta_two * m2_ref[p] + (1.0 - beta_two) * grad * grad
        n1_ref[p] = one
        n2_ref[p] = two
        update = one / (jnp.sqrt(two) + epsilon) + weight_decay * weight
        update_ref[p] = update
        sums.append(jnp.sum(weight * weight, axis=0, keepdims=True))
        sums.append(jnp.sum(update * update, axis=0, keepdims=True))
    a_msg[...] = jnp.concatenate(sums + [jnp.zeros((4, DIM), F32)], axis=0)
    a_in[member] = a_msg[...]
    for i, peer in enumerate(members):
        copies.append(send(a_msg, a_in.at[member], a_send.at[i], a_recv.at[member], peer))

    for i in range(1, GROUP):
        slot = lax.rem(member + i, GROUP)
        arrived(a_in.at[slot], a_recv.at[slot])
    summed = a_in[0]
    for slot in range(1, GROUP):
        summed = summed + a_in[slot]
    b_msg[...] = summed
    b_in[line] = summed
    late = [
        send(b_msg, b_in.at[line], b_send.at[i], b_recv.at[line], peer)
        for i, peer in enumerate(lines)
    ]
    for copy in copies:
        copy.wait_send()
    for p in range(2):
        for i in range(1, OWNERS):
            to_owner(p, i).wait_send()

        @pl.when(jnp.logical_not(here))
        def _():
            to_owner(p, 0).wait_send()

    for i in range(1, OWNERS):
        slot = lax.rem(line + i, OWNERS)
        arrived(b_in.at[slot], b_recv.at[slot])
    summed = b_in[0]
    for slot in range(1, OWNERS):
        summed = summed + b_in[slot]
    norms = jnp.sqrt(jnp.sum(summed, axis=1, keepdims=True))
    ratios = []
    for p in range(2):
        ratio = norms[2 * p:2 * p + 1] / (norms[2 * p + 1:2 * p + 2] + epsilon)
        ratios.append(ratio)
    trust_ref[...] = jnp.concatenate(
        [jnp.broadcast_to(ratio, (1, DIM)) for ratio in ratios] + [jnp.zeros((6, DIM), F32)], axis=0
    )
    for copy in late:
        copy.wait_send()


def whole(span_order, queries, out_grad, attn_out, key_states, value_states, act, segment_ids,
          kv_weight, moment_one, moment_two):
    state = jax.ShapeDtypeStruct((2, 32, DIM), F32)
    dma = pltpu.SemaphoreType.DMA
    return pl.pallas_call(
        whole_kernel,
        out_shape=(
            jax.ShapeDtypeStruct((ROWS, HEADS * DIM), BF16),
            jax.ShapeDtypeStruct((ROWS, 2 * DIM), BF16),
            state, state, state,
            jax.ShapeDtypeStruct((8, DIM), F32),
        ),
        in_specs=[smem_spec()] + [any_spec()] * 6 + [vmem_spec()] + [any_spec()] * 3,
        out_specs=(vmem_spec(),) * 6,
        scratch_shapes=[
            VMEM((2, 32, DIM), F32),
            VMEM((2, 32, DIM), F32),
            VMEM((2, 32, DIM), F32),
            VMEM((ROWS, HEADS * DIM), BF16),
            VMEM((ROWS, HEADS * DIM), BF16),
            VMEM((ROWS, HEADS * DIM), BF16),
            VMEM((8, LANES, DIM), BF16),
            VMEM((8, LANES, DIM), BF16),
            VMEM((16, ROWS, DIM), BF16),
            VMEM((16, ROWS, DIM), BF16),
            VMEM((4, 8, LANES), F32),
            VMEM((4, 8, LANES), F32),
            VMEM((16, 8, ROWS), F32),
            VMEM((KEYS, 2 * DIM), BF16),
            VMEM((KEYS, 2 * DIM), BF16),
            VMEM((8, 2 * DIM, LANES), BF16),
            VMEM((8, 2 * DIM, LANES), BF16),
            VMEM((KEYS // BLOCK, DIM, BLOCK), BF16),
            VMEM((KEYS, LANES), F32),
            VMEM((2, 8, LANES), F32),
            VMEM((4, 2, 8, LANES), F32),
            VMEM((BLOCK, DIM), F32),
            VMEM((BLOCK, DIM), F32),
            VMEM((8, DIM, LANES), F32),
            VMEM((16, 2, ROWS, DIM), BF16),
            VMEM((16, 2, ROWS, DIM), BF16),
            VMEM((8, LANES, DIM), BF16),
            VMEM((4, 2, LANES, DIM), BF16),
            VMEM((GROUP, ROWS, FEATURES), BF16),
            VMEM((2, GROUP, ROWS, DIM), BF16),
            VMEM((2, FEATURES, DIM), BF16),
            VMEM((2, OWNERS, 32, DIM), BF16),
            VMEM((GROUP, 8, DIM), F32),
            VMEM((8, DIM), F32),
            VMEM((OWNERS, 8, DIM), F32),
            VMEM((8, DIM), F32),
            dma((4, 3)), dma((4, 4)),
            dma((3, 15)), dma((3, 16)),
            dma((7,)), dma((7,)),
            dma((3,)), dma((4,)),
            dma((15,)), dma((16,)),
            dma((3,)), dma((4,)),
            dma((2, 7)), dma((2, 7)),
            dma((2, OWNERS)), dma((2, OWNERS)),
            dma((7,)), dma((GROUP,)),
            dma((31,)), dma((OWNERS,)),
            dma((9,)),
        ],
        compiler_params=pltpu.CompilerParams(
            collective_id=0, has_side_effects=True, vmem_limit_bytes=VMEM_LIMIT
        ),
        name="attention_backward",
    )(span_order, queries, out_grad, attn_out, key_states, value_states, act, segment_ids,
      kv_weight, moment_one, moment_two)


def finish_kernel(
    q_ref, kv_ref, update_ref, one_ref, two_ref, ratio_ref, weight_ref,
    qgrad_ref, kvgrad_ref, nw_ref, n1_ref, n2_ref, trust_ref,
):
    qgrad_ref[0] = q_ref[...]
    kvgrad_ref[0] = kv_ref[...]
    n1_ref[...] = one_ref[...]
    n2_ref[...] = two_ref[...]
    for p in range(2):
        ratio = ratio_ref[pl.ds(p, 1), :]
        trust_ref[p] = ratio[0, 0]
        nw_ref[p] = weight_ref[p] - learn_rate * ratio * update_ref[p]


def finish(query_grad, kv_grad, update, new_one, new_two, ratio, kv_weight):
    state = jax.ShapeDtypeStruct((2, 32, DIM), F32)
    return pl.pallas_call(
        finish_kernel,
        out_shape=(
            jax.ShapeDtypeStruct((1, ROWS, HEADS * DIM), BF16),
            jax.ShapeDtypeStruct((1, ROWS, 2 * DIM), BF16),
            state, state, state,
            jax.ShapeDtypeStruct((2,), F32),
        ),
        in_specs=[vmem_spec()] * 7,
        out_specs=(vmem_spec(),) * 5 + (smem_spec(),),
        compiler_params=pltpu.CompilerParams(vmem_limit_bytes=VMEM_LIMIT),
        name="new_weights",
    )(query_grad, kv_grad, update, new_one, new_two, ratio, kv_weight)


def on_device(
    queries,
    key_states,
    value_states,
    attn_out,
    out_grad,
    activations,
    segment_ids,
    span_order,
    kv_weight,
    moment_one,
    moment_two,
):
    query_grad, kv_grad, update, new_one, new_two, trust = whole(
        span_order, queries[0], out_grad[0], attn_out[0], key_states[0], value_states[0],
        activations[0], segment_ids, kv_weight, moment_one, moment_two,
    )
    return finish(query_grad, kv_grad, update, new_one, new_two, trust, kv_weight)


def solution(mesh):
    in_specs = (
        P("dp", "context", None),
        P("dp", "context", None),
        P("dp", "context", None),
        P("dp", "context", None),
        P("dp", "context", None),
        P("dp", "context", None),
        P("dp", "context"),
        P(),
        P(None, ("context", "dp"), None),
        P(None, ("context", "dp"), None),
        P(None, ("context", "dp"), None),
    )
    out_specs = (
        P("dp", "context", None),
        P("dp", "context", None),
        P(None, ("context", "dp"), None),
        P(None, ("context", "dp"), None),
        P(None, ("context", "dp"), None),
        P(),
    )
    return jax.shard_map(
        on_device, mesh=mesh, in_specs=in_specs, out_specs=out_specs, check_vma=False
    )
```
